512 devices in a mesh: prow: 16 (over y, core), pcol: 32 (over x, z).
Axes of the slice: x: 4, y: 8, z: 8, core: 2. Of those that a mesh axis runs over, the one named last changes fastest.
Arguments:
- rhs: float32 [6, 16, 64, 128], P(None, 'prow'), may hold values from -6 to 6
- lower: float32 [6, 16, 3, 32, 128, 128], P(None, 'prow', None, 'pcol'), may hold values from -0.125 to 0.125
- lower_pattern: int32 [6, 16, 3, 32], P(None, 'prow', None, 'pcol'), may hold values from 0 to 1, as said below
- lower_inv: float32 [6, 16, 128, 128], P(None, 'prow')
- upper: float32 [6, 16, 3, 32, 128, 128], P(None, 'prow', None, 'pcol'), may hold values from -0.125 to 0.125
- upper_pattern: int32 [6, 16, 3, 32], P(None, 'prow', None, 'pcol'), may hold values from 0 to 1, as said below
- upper_inv: float32 [6, 16, 128, 128], P(None, 'prow')
Outputs:
- solution: float32 [6, 16, 64, 128], P(None, 'prow')
The draws below stay inside these ranges and needn't reach their ends.
Inputs may be any that keep to these rules, and one draw needn't show every extreme that they name: `lower_pattern`: 1 only where the column block descends from the row block in the elimination tree. `upper_pattern`: 1 only where the row block descends from the column block in the elimination tree.
All inputs are finite; a program needn't handle non-finite values.
Results may differ from the reference program's by a relative error of at most 0.00014.
Values sent between devices are 32-bit elements; how exact they have to be, the bound alone decides.
A program may use at most 64 MiB of HBM per device.

```python
import jax
import jax.numpy as jnp
from jax import lax

B = 128
K = 64
NLEV = 6
PROWS = 16
PCOLS = 32
NBLK = 96
MCOL = 3


def level_grid():
    row_level = jnp.arange(NLEV, dtype=jnp.int32)[:, None, None, None]
    row_place = jnp.arange(PROWS, dtype=jnp.int32)[None, :, None, None]
    column = jnp.arange(MCOL, dtype=jnp.int32)[None, None, :, None] * PCOLS + jnp.arange(PCOLS, dtype=jnp.int32)[None, None, None, :]
    return (row_level, row_place, column // PROWS, column % PROWS)


def same_subtree(place_a, place_b, level):
    width = jnp.left_shift(jnp.ones_like(level), level)
    return place_a // width == place_b // width


def draw_lower_pattern(key, part):
    key = jax.random.fold_in(key, 11)
    row_level, row_place, col_level, col_place = level_grid()
    coins = (jax.random.randint(key, (NLEV, PROWS, MCOL, PCOLS), 0, 4) > 0).astype(jnp.int32)
    below = jnp.logical_and(col_level < row_level, same_subtree(row_place, col_place, row_level))
    return (coins * below.astype(jnp.int32)).astype(jnp.int32)


def draw_upper_pattern(key, part):
    key = jax.random.fold_in(key, 12)
    row_level, row_place, col_level, col_place = level_grid()
    coins = (jax.random.randint(key, (NLEV, PROWS, MCOL, PCOLS), 0, 4) > 0).astype(jnp.int32)
    above = jnp.logical_and(col_level > row_level, same_subtree(row_place, col_place, col_level))
    return (coins * above.astype(jnp.int32)).astype(jnp.int32)


def dominant(key):
    first, second = jax.random.split(key)
    diag = jax.random.uniform(first, (NLEV, PROWS, B), jnp.float32, 0.6, 1.4)
    off = jax.random.normal(second, (NLEV, PROWS, B, B), jnp.float32) * (0.5 / B ** 0.5)
    eye = jnp.eye(B, dtype=jnp.float32)
    return off * (1.0 - eye) + eye * diag[:, :, :, None]


def draw_lower_inv(key, part):
    key = jax.random.fold_in(key, 21)
    return dominant(key)


def draw_upper_inv(key, part):
    key = jax.random.fold_in(key, 22)
    return dominant(key)


def levels(own_key, dims, pieces, smallest, high):
    factor_of, own = 1.0, jax.random.fold_in(own_key, 6)
    for dim, shards_of in pieces:
        heights = jnp.exp(jax.random.uniform(jax.random.fold_in(own, dim), (shards_of,), jnp.float32, smallest / len(pieces), high / len(pieces)))
        factor_of = factor_of * jnp.repeat(heights, dims[dim] // shards_of).reshape([-1 if axis == dim else 1 for axis in range(len(dims))])
    return factor_of


def bell_draw(key, shape, scale, limit, shards=(), kind=jnp.bfloat16):
    drawn = scale * jax.random.normal(key, shape, jnp.float32)
    if shards:
        drawn = drawn * levels(key, shape, shards, -0.22, 0.18)
    return jnp.clip(drawn, -limit, limit).astype(kind)


def setup_inputs(seed: int = 0) -> dict:
    arg_keys = jax.random.split(jax.random.key(seed), 8)
    rhs = bell_draw(arg_keys[0], (NLEV, PROWS, K, B), 1.0, 6.0, ((1, 16),), jnp.float32)
    lower = bell_draw(arg_keys[1], (NLEV, PROWS, MCOL, PCOLS, B, B), (B * PROWS) ** -0.5, 0.125, ((1, 16), (3, 32)), jnp.float32)
    lower_pattern = draw_lower_pattern(jax.random.fold_in(arg_keys[7], 71), 0)
    lower_inv = draw_lower_inv(jax.random.fold_in(arg_keys[7], 71), 0)
    upper = bell_draw(arg_keys[4], (NLEV, PROWS, MCOL, PCOLS, B, B), (B * PROWS) ** -0.5, 0.125, ((1, 16), (3, 32)), jnp.float32)
    upper_pattern = draw_upper_pattern(jax.random.fold_in(arg_keys[7], 71), 0)
    upper_inv = draw_upper_inv(jax.random.fold_in(arg_keys[7], 71), 0)
    return dict(rhs=rhs, lower=lower, lower_pattern=lower_pattern, lower_inv=lower_inv, upper=upper, upper_pattern=upper_pattern, upper_inv=upper_inv)


def sweep(right, blocks, pattern, inverse, order):
    solved = jnp.zeros((NBLK, K, B), jnp.float32)
    for level in order:
        masked = blocks[level] * pattern[level].astype(jnp.float32)[:, :, :, None, None]
        known = solved.reshape(MCOL, PCOLS, K, B)
        partial_value = jnp.einsum("pmcij,mckj->pki", masked, known, precision=lax.Precision.HIGHEST)
        current = right[level] - partial_value
        value = jnp.einsum("pij,pkj->pki", inverse[level], current, precision=lax.Precision.HIGHEST)
        solved = solved.at[level * PROWS:(level + 1) * PROWS].set(value)
    return solved.reshape(NLEV, PROWS, K, B)


def reference(rhs, lower, lower_pattern, lower_inv, upper, upper_pattern, upper_inv):
    forward = sweep(rhs, lower, lower_pattern, lower_inv, list(range(NLEV)))
    return sweep(forward, upper, upper_pattern, upper_inv, list(range(NLEV - 1, -1, -1)))
```

```python
import functools

import jax
import jax.numpy as jnp
from jax import lax
from jax.experimental import pallas as pl
from jax.experimental.pallas import tpu as pltpu
from jax.sharding import PartitionSpec as P

MESH = pl.DeviceIdType.MESH
NL = 6
NP = 16
NS = 8
F32 = jnp.float32


def mm_t(x, w):
    return lax.dot_general(
        x, w, (((1,), (1,)), ((), ())),
        precision=lax.Precision.HIGHEST, preferred_element_type=F32,
    )


def mm(a, b):
    return lax.dot_general(
        a, b, (((1,), (0,)), ((), ())),
        precision=lax.Precision.HIGHEST, preferred_element_type=F32,
    )


def width(level):
    return min(NP, 1 << level)


def kernel(
    lpat, upat, rhs_h, low_h, linv_h, upp_h, uinv_h, out,
    rhs, low, linv, upp, uinv, mf, mb, accf, accb, xf, xb, pf, pb, ca, cb, da, db, own,
    s_in, s_x, s_z, s_ca, s_cb, s_da, s_db, s_out, t_x0, t_a, t_b, t_ag, t_out,
):
    r = lax.axis_index("prow")
    c = lax.axis_index("pcol")
    par, q = c // NP, lax.rem(c, NP)
    even, odd = par == 0, par == 1
    yr, yq = r // 2, q // 2
    dy = lax.rem(yr - yq + 9, 8)
    owner = dy < 4
    slot = jnp.where(owner, dy * 2 + lax.rem(r, 2), 0)
    diag = r == q

    def same(level):
        return r // width(level) == q // width(level)

    def near(position, j):
        return lax.rem(position // 2 + j // 2 + 7, 8) * 2 + lax.rem(j, 2)

    def at(row, parity, col):
        return {"prow": row, "pcol": parity * NP + col}

    barrier = pltpu.get_barrier_semaphore()

    def tell(device):
        pl.semaphore_signal(barrier, inc=1, device_id=device, device_id_type=MESH)

    @pl.loop(0, NS)
    def _(j):
        s = near(r, j)
        tell(at(s, 1 - par, r))

        @pl.when(jnp.logical_not(jnp.logical_and(diag, s == r)))
        def _():
            tell(at(s, par, r))

        s2 = near(q, j)

        @pl.when(s2 != r)
        def _():
            tell(at(s2, par, q))

    @pl.when(owner)
    def _():
        @pl.loop(0, NP)
        def _(k):
            tell(at(q, 1 - par, k))

            @pl.when(jnp.logical_not(jnp.logical_and(diag, k == q)))
            def _():
                tell(at(q, par, k))

    loads = [
        (rhs_h, rhs), (linv_h, linv), (uinv_h, uinv),
    ]
    for m in range(3):
        loads.append((low_h.at[pl.ds(2 * m + 1, 5 - 2 * m), m], low.at[pl.ds(2 * m + 1, 5 - 2 * m), m]))
    for m in range(3):
        loads.append((upp_h.at[pl.ds(0, 2 * m + 1), m], upp.at[pl.ds(0, 2 * m + 1), m]))
    copies = [pltpu.make_async_copy(a, b, s_in.at[i]) for i, (a, b) in enumerate(loads)]
    for copy in copies:
        copy.start()

    accf[...] = jnp.zeros_like(accf)
    accb[...] = jnp.zeros_like(accb)
    for copy in copies[:6]:
        copy.wait()

    top = mm(uinv[5], linv[5])

    def fold(inv, block, bit):
        return mm(inv, block * bit.astype(F32))

    for m in range(3):
        for row in range(2 * m + 1, NL):
            mf[row, m] = fold(top if row == 5 else linv[row], low[row, m], lpat[row, m])

    @pl.when(diag)
    def _():
        for row in range(1, NL):
            @pl.when(par == (row - 1) % 2)
            def _(row=row):
                accf[row] = mm_t(rhs[row], top if row == 5 else linv[row]).reshape(NS, 8, 128)

        @pl.when(even)
        def _():
            xf[0] = mm_t(rhs[0], linv[0]).reshape(NS, 8, 128)

    to_self = jnp.where(diag, 1, 0)
    pl.semaphore_wait(barrier, jnp.where(owner, NP - 1 + 2 * NP + 2 * NS - 2 * to_self, 2 * NS))

    @pl.when(jnp.logical_and(diag, even))
    def _():
        @pl.loop(1, NP)
        def _(d):
            pltpu.make_async_remote_copy(
                xf.at[0], xf.at[0], t_x0.at[d], s_x.at[0],
                device_id=at(jnp.bitwise_xor(r, d), par, q), device_id_type=MESH,
            ).start()

    def send_slices(source, target, place, send_sem, recv_sem, parity):
        for j in range(NS):
            s = near(r, j)

            def remote(j=j, s=s):
                pltpu.make_async_remote_copy(
                    source.at[j], target.at[place], send_sem, recv_sem,
                    device_id=at(s, parity, r), device_id_type=MESH,
                ).start()

            if parity is par:
                me = jnp.logical_and(diag, s == r)
                pl.when(jnp.logical_not(me))(remote)

                @pl.when(me)
                def _(j=j):
                    pltpu.make_async_copy(source.at[j], target.at[place], recv_sem).start()
            else:
                remote()

    def wait_bytes(ref, sem):
        pltpu.make_async_copy(ref, ref, sem).wait()

    def wait_sent_slices(source, send_sem, same_parity):
        if not same_parity:
            wait_bytes(source, send_sem)
            return

        @pl.when(diag)
        def _():
            wait_bytes(source.at[pl.ds(0, NS - 1)], send_sem)

        @pl.when(jnp.logical_not(diag))
        def _():
            wait_bytes(source, send_sem)

    def wait_slices(ref, sem):
        @pl.when(owner)
        def _():
            wait_bytes(ref.at[pl.ds(0, NS - 1)], sem)

        @pl.when(jnp.logical_not(owner))
        def _():
            wait_bytes(ref, sem)

    def spread(level, store, sem, wide):
        @pl.loop(1, wide + 1 if wide < NP else NP)
        def _(d):
            if wide == NP:
                row = jnp.bitwise_xor(r, d)
            else:
                row = q // wide * wide + d - 1

            @pl.when(row != r)
            def _():
                pltpu.make_async_remote_copy(
                    own.at[level], store.at[level, slot], t_ag.at[level], sem.at[level],
                    device_id=at(row, par, q), device_id_type=MESH,
                ).start()

    def deliver(level):
        @pl.loop(0, NP)
        def _(k):
            pltpu.make_async_remote_copy(
                own.at[NL + level], out.at[level, slot], t_out.at[level], s_out,
                device_id=at(q, 1 - par, k), device_id_type=MESH,
            ).start()
            me = jnp.logical_and(diag, k == q)

            @pl.when(jnp.logical_not(me))
            def _():
                pltpu.make_async_remote_copy(
                    own.at[NL + level], out.at[level, slot], t_out.at[level], s_out,
                    device_id=at(q, par, k), device_id_type=MESH,
                ).start()

            @pl.when(me)
            def _():
                pltpu.make_async_copy(own.at[NL + level], out.at[level, slot], s_out).start()

    def forward_hold(level):
        m = level // 2
        if level == 0:
            @pl.when(jnp.logical_not(diag))
            def _():
                wait_bytes(xf.at[0], s_x.at[0])
        else:
            wait_slices(xf.at[level], s_x.at[level])
        x = xf[level].reshape(64, 128)

        @pl.when(same(level + 1))
        def _():
            pf[level] = accf[level + 1] - mm_t(x, mf[level + 1, m]).reshape(NS, 8, 128)
            send_slices(pf.at[level], ca, (level + 1) * NP + lax.rem(q, width(level + 1)), t_a.at[level + 1], s_ca.at[level + 1], 1 - par)

        for row in range(level + 2, NL):
            @pl.when(same(row))
            def _(row=row):
                accf[row] = accf[row] - mm_t(x, mf[row, m]).reshape(NS, 8, 128)
                if row == level + 2:
                    send_slices(accf.at[row], cb, row * NP + lax.rem(q, width(row)), t_b.at[row], s_cb.at[row], par)

        @pl.when(diag)
        def _():
            accb[level] = mm_t(x, uinv[level]).reshape(NS, 8, 128)
            if level == 4:
                send_slices(accb.at[4], db, 4 * NP, t_b.at[NL + 4], s_db.at[4], par)

    def forward_own(level):
        n = width(level)
        wait_bytes(ca.at[pl.ds(level * NP, n)], s_ca.at[level])
        total = jnp.sum(ca[level * NP:level * NP + n], axis=0)
        if level >= 2:
            wait_bytes(cb.at[pl.ds(level * NP, n)], s_cb.at[level])
            total = total + jnp.sum(cb[level * NP:level * NP + n], axis=0)
        if level == 5:
            own[NL + 5] = total
            own[5] = total
            xb[5, slot] = total
            spread(5, xb, s_z, NP)
            deliver(5)
        else:
            own[level] = total
            xf[level, slot] = total
            spread(level, xf, s_x, NP)

    def back_hold(level):
        m = level // 2
        row = level - 1

        @pl.when(same(level))
        def _():
            wait_slices(xb.at[level], s_z.at[level])
            z = xb[level].reshape(64, 128)
            pb[row] = accb[row] - mm_t(z, mb[row, m]).reshape(NS, 8, 128)

        @pl.when(jnp.logical_not(same(level)))
        def _():
            pb[row] = accb[row]

        send_slices(pb.at[row], da, row * NP + q, t_a.at[NL + row], s_da.at[row], 1 - par)

        if level >= 2:
            @pl.when(same(level))
            def _():
                z = xb[level].reshape(64, 128)
                for lower in range(level - 2, -1, -1):
                    accb[lower] = accb[lower] - mm_t(z, mb[lower, m]).reshape(NS, 8, 128)
            send_slices(accb.at[level - 2], db, (level - 2) * NP + q, t_b.at[NL + level - 2], s_db.at[level - 2], par)

    def back_own(level):
        wait_bytes(da.at[pl.ds(level * NP, NP)], s_da.at[level])
        total = jnp.sum(da[level * NP:level * NP + NP], axis=0)
        n = 1 if level == 4 else NP
        wait_bytes(db.at[pl.ds(level * NP, n)], s_db.at[level])
        total = total + jnp.sum(db[level * NP:level * NP + n], axis=0)
        own[NL + level] = total
        if level > 0:
            @pl.when(same(level))
            def _():
                xb[level, slot] = total
            spread_back(level)
        deliver(level)

    def spread_back(level):
        wide = width(level)

        @pl.loop(0, wide)
        def _(d):
            row = q // wide * wide + d

            @pl.when(row != r)
            def _():
                pltpu.make_async_remote_copy(
                    own.at[NL + level], xb.at[level, slot], t_ag.at[NL + level], s_z.at[level],
                    device_id=at(row, par, q), device_id_type=MESH,
                ).start()

    def prepare_back():
        for copy in copies[6:]:
            copy.wait()
        for m in range(3):
            for row in range(0, 2 * m + 1):
                mb[row, m] = fold(uinv[row], upp[row, m], upat[row, m])

    def run(parity):
        first = True
        for level in range(NL):
            if level % 2 == parity:
                if level > 0:
                    pl.when(owner)(functools.partial(forward_own, level))
                if level < 5:
                    forward_hold(level)
                if first:
                    prepare_back()
                    first = False
        for level in range(NL - 1, -1, -1):
            if level % 2 == parity:
                if level < 5:
                    pl.when(owner)(functools.partial(back_own, level))
                if level > 0:
                    back_hold(level)

    @pl.when(even)
    def _():
        run(0)

    @pl.when(odd)
    def _():
        run(1)

    @pl.when(jnp.logical_and(diag, even))
    def _():
        @pl.loop(1, NP)
        def _(d):
            wait_bytes(xf.at[0], t_x0.at[d])

    for level in range(NL):
        if level < 5:
            @pl.when(jnp.logical_and(par == level % 2, same(level + 1)))
            def _(level=level):
                wait_sent_slices(pf.at[level], t_a.at[level + 1], False)
            if level + 2 < NL:
                @pl.when(jnp.logical_and(par == level % 2, same(level + 2)))
                def _(level=level):
                    wait_sent_slices(accf.at[level + 2], t_b.at[level + 2], True)
        if level > 0:
            @pl.when(par == level % 2)
            def _(level=level):
                wait_sent_slices(pb.at[level - 1], t_a.at[NL + level - 1], False)
                if level >= 2:
                    wait_sent_slices(accb.at[level - 2], t_b.at[NL + level - 2], True)

    @pl.when(jnp.logical_and(diag, even))
    def _():
        wait_sent_slices(accb.at[4], t_b.at[NL + 4], True)

    @pl.when(owner)
    def _():
        for level in range(NL):
            @pl.when(par == level % 2)
            def _(level=level):
                if level > 0:
                    wait_bytes(da.at[pl.ds(0, NP - 1)], t_ag.at[level])
                if 0 < level < 5:
                    @pl.when(same(level))
                    def _():
                        if width(level) > 1:
                            wait_bytes(da.at[pl.ds(0, width(level) - 1)], t_ag.at[NL + level])

                    @pl.when(jnp.logical_not(same(level)))
                    def _():
                        wait_bytes(da.at[pl.ds(0, width(level))], t_ag.at[NL + level])

                @pl.when(diag)
                def _():
                    wait_bytes(da.at[pl.ds(0, 2 * NP - 1)], t_out.at[level])

                @pl.when(jnp.logical_not(diag))
                def _():
                    wait_bytes(da.at[pl.ds(0, 2 * NP)], t_out.at[level])

    wait_bytes(out, s_out)


def shards(rhs, lower, lower_pattern, lower_inv, upper, upper_pattern, upper_inv):
    v = pltpu.VMEM
    dma = pltpu.SemaphoreType.DMA
    slices = (NL, NS, 8, 128)
    parts = (NL * NP, 8, 128)
    blocks = (NL, 3, 128, 128)
    got = pl.pallas_call(
        kernel,
        out_shape=jax.ShapeDtypeStruct(slices, F32),
        in_specs=[pl.BlockSpec(memory_space=pltpu.SMEM)] * 2 + [pl.BlockSpec(memory_space=pl.ANY)] * 5,
        out_specs=pl.BlockSpec(memory_space=pltpu.VMEM),
        scratch_shapes=[
            v((NL, 64, 128), F32), v(blocks, F32), v((NL, 128, 128), F32), v(blocks, F32), v((NL, 128, 128), F32),
            v(blocks, F32), v(blocks, F32), v(slices, F32), v(slices, F32), v(slices, F32), v(slices, F32),
            v(slices, F32), v(slices, F32), v(parts, F32), v(parts, F32), v(parts, F32), v(parts, F32),
            v((2 * NL, 8, 128), F32),
            dma((9,)), dma((NL,)), dma((NL,)), dma((NL,)), dma((NL,)), dma((NL,)), dma((NL,)), dma,
            dma((NP,)), dma((2 * NL,)), dma((2 * NL,)), dma((2 * NL,)), dma((NL,)),
        ],
        compiler_params=pltpu.CompilerParams(
            collective_id=0, has_side_effects=True, vmem_limit_bytes=32 * 1024 * 1024
        ),
        name="substitution",
    )(
        lower_pattern.reshape(NL, 3), upper_pattern.reshape(NL, 3), rhs.reshape(NL, 64, 128),
        lower.reshape(blocks), lower_inv.reshape(NL, 128, 128), upper.reshape(blocks), upper_inv.reshape(NL, 128, 128),
    )
    return got.reshape(NL, 1, 64, 128)


def solution(mesh):
    in_specs = (
        P(None, "prow", None, None),
        P(None, "prow", None, "pcol", None, None),
        P(None, "prow", None, "pcol"),
        P(None, "prow", None, None),
        P(None, "prow", None, "pcol", None, None),
        P(None, "prow", None, "pcol"),
        P(None, "prow", None, None),
    )
    out_specs = P(None, "prow", None, None)
    return jax.shard_map(shards, mesh=mesh, in_specs=in_specs, out_specs=out_specs, check_vma=False)
```

```python
import functools

import jax
import jax.numpy as jnp
from jax import lax
from jax.experimental import pallas as pl
from jax.experimental.pallas import tpu as pltpu
from jax.sharding import PartitionSpec as P

MESH = pl.DeviceIdType.MESH
NL = 6
NP = 16
NS = 8
BF16 = jnp.bfloat16
F32 = jnp.float32


def mm_t(x, w):
    return lax.dot_general(
        x, w, (((1,), (1,)), ((), ())),
        precision=lax.Precision.HIGHEST, preferred_element_type=F32,
    )


def mm(a, b):
    return lax.dot_general(
        a, b, (((1,), (0,)), ((), ())),
        precision=lax.Precision.HIGHEST, preferred_element_type=F32,
    )


HELD = {}
for _row, _col in ((5, 4), (4, 5), (3, 4), (2, 3), (1, 3), (0, 3), (1, 2), (0, 2), (0, 1)):
    HELD[_row, _col] = (sum(n for _, n in HELD.values()), min(NP, 1 << _col))
NHELD = sum(n for _, n in HELD.values())
GROUP = {key: i for i, key in enumerate(HELD)}
GATHERED = {"x4": (0, 16), "z5": (16, 16), "z4": (32, 16), "z3": (48, 8), "z2": (56, 4), "z1": (60, 2)}
STEP = {key: i for i, key in enumerate(GATHERED)}
NGATHERED = 62


def split(x):
    high = x.astype(BF16)
    return high, (x - high.astype(F32)).astype(BF16)


def dot_t(x, w):
    return lax.dot_general(x, w, (((1,), (1,)), ((), ())), preferred_element_type=F32)


def width(level):
    return min(NP, 1 << level)


def kernel(
    lpat, upat, rhs_h, low_h, linv_h, upp_h, uinv_h, out,
    rhs, low, linv, upp, uinv, mf, mb, accf, accb, xf, xb, pf, ca, cb, own,
    held, wh, wl, seen, mine, r4, r5, r45, d3, d5, d4,
    s_in, s_x, s_z, s_ca, s_cb, s_held, s_seen, s_rows, s_out,
    t_x0, t_a, t_b, t_ag, t_held, t_seen, t_rows, t_z, t_out,
):
    r = lax.axis_index("prow")
    c = lax.axis_index("pcol")
    par, q = c // NP, lax.rem(c, NP)
    even, odd = par == 0, par == 1
    dy = lax.rem(r // 2 - q // 2 + 9, 8)
    owner = dy < 4
    slot = jnp.where(owner, dy * 2 + lax.rem(r, 2), 0)
    diag = r == q
    col_x, col_z = c // 8, lax.rem(c, 8)
    turned = lax.rem(col_z + 8 - 2 * lax.rem(col_x, 2), 8)
    team = lax.rem(turned, 4) == 0
    k_me = jnp.where(team, col_x * 2 + turned // 4, 0)

    def seat(k):
        return 8 * (k // 2) + 4 * lax.rem(k, 2) + 2 * lax.rem(k // 2, 2)

    def same(level):
        return r // width(level) == q // width(level)

    def near(position, j):
        return lax.rem(position // 2 + j // 2 + 7, 8) * 2 + lax.rem(j, 2)

    def at(row, col):
        return {"prow": row, "pcol": col}

    barrier = pltpu.get_barrier_semaphore()

    def tell(row, col):
        @pl.when(jnp.logical_not(jnp.logical_and(row == r, col == c)))
        def _():
            pl.semaphore_signal(barrier, inc=1, device_id=at(row, col), device_id_type=MESH)

    @pl.loop(0, NS)
    def _(j):
        tell(near(q, j), c)
        tell(r, seat(j))
        tell(q, seat(j))

    @pl.when(owner)
    def _():
        @pl.loop(0, 2 * NP)
        def _(k):
            tell(q, k)

    @pl.when(team)
    def _():
        @pl.loop(0, 2 * NP)
        def _(k):
            tell(r, k)

        @pl.loop(0, NP)
        def _(k):
            tell(k, c)

    loads = [(rhs_h, rhs), (linv_h, linv), (uinv_h, uinv)]
    for m in range(3):
        loads.append((low_h.at[pl.ds(2 * m + 1, 5 - 2 * m), m], low.at[pl.ds(2 * m + 1, 5 - 2 * m), m]))
    for m in range(3):
        loads.append((upp_h.at[pl.ds(0, 2 * m + 1), m], upp.at[pl.ds(0, 2 * m + 1), m]))
    copies = [pltpu.make_async_copy(a, b, s_in.at[i]) for i, (a, b) in enumerate(loads)]
    for copy in copies:
        copy.start()

    accf[...] = jnp.zeros_like(accf)
    accb[...] = jnp.zeros_like(accb)
    for copy in copies[:6]:
        copy.wait()

    top = mm(uinv[5], linv[5])

    def fold(inv, block, bit):
        return mm(inv, block * bit.astype(F32))

    for m in range(3):
        for row in range(2 * m + 1, NL):
            mf[row, m] = fold(top if row == 5 else linv[row], low[row, m], lpat[row, m])

    @pl.when(diag)
    def _():
        for row in range(1, NL):
            @pl.when(par == (row - 1) % 2)
            def _(row=row):
                accf[row] = mm_t(rhs[row], top if row == 5 else linv[row]).reshape(NS, 8, 128)

        @pl.when(even)
        def _():
            xf[0] = mm_t(rhs[0], linv[0]).reshape(NS, 8, 128)

    one = jnp.where(diag, 1, 0)
    sat = jnp.where(team, 1, 0)
    expected = 2 * NS - one + jnp.where(owner, NP - 1, 0) + NS - sat
    expected = expected + jnp.where(team, 2 * NP - 1 + NP - 1 + 2 * NP - one, 0)
    pl.semaphore_wait(barrier, expected)

    def wait_bytes(ref, sem):
        pltpu.make_async_copy(ref, ref, sem).wait()

    def push(source, target, send_sem, recv_sem, row, col, may_be_me):
        def remote():
            pltpu.make_async_remote_copy(
                source, target, send_sem, recv_sem, device_id=at(row, col), device_id_type=MESH
            ).start()

        if not may_be_me:
            remote()
            return
        me = jnp.logical_and(row == r, col == c)
        pl.when(jnp.logical_not(me))(remote)

        @pl.when(me)
        def _():
            pltpu.make_async_copy(source, target, recv_sem).start()

    @pl.when(jnp.logical_and(diag, even))
    def _():
        @pl.loop(1, NP)
        def _(d):
            push(xf.at[0], xf.at[0], t_x0.at[d], s_x.at[0], jnp.bitwise_xor(r, d), c, False)

    def to_owners(source, target, place, send_sem, recv_sem, parity):
        for j in range(NS):
            push(source.at[j], target.at[place], send_sem, recv_sem, near(r, j), parity * NP + r, parity is par)

    def to_team(piece, target, send_sem, recv_sem):
        for k in range(NS):
            push(piece(k), target, send_sem, recv_sem, r, seat(k), True)

    def wait_slices(ref, sem):
        @pl.when(owner)
        def _():
            wait_bytes(ref.at[pl.ds(0, NS - 1)], sem)

        @pl.when(jnp.logical_not(owner))
        def _():
            wait_bytes(ref, sem)

    def give(row, col, source):
        first, n = HELD[row, col]
        i = GROUP[row, col]

        @pl.when(same(col))
        def _():
            @pl.loop(0, NS)
            def _(k):
                push(source, held.at[first + lax.rem(q, n)], t_held.at[i], s_held.at[i], r, seat(k), True)

    def minus(ref, row, x, w):
        ref[row] = ref[row] - mm_t(x, w).reshape(NS, 8, 128)

    def forward_hold(level):
        m = level // 2
        if level == 0:
            @pl.when(jnp.logical_not(diag))
            def _():
                wait_bytes(xf.at[0], s_x.at[0])
        else:
            wait_slices(xf.at[level], s_x.at[level])
        x = xf[level].reshape(64, 128)
        if level < 3:
            @pl.when(same(level + 1))
            def _():
                row = level + 1
                pf[level] = accf[row] - mm_t(x, mf[row, m]).reshape(NS, 8, 128)
                to_owners(pf.at[level], ca, row * NP + lax.rem(q, width(row)), t_a.at[row], s_ca.at[row], 1 - par)

            row = level + 2
            if row < 4:
                @pl.when(same(row))
                def _():
                    minus(accf, row, x, mf[row, m])
                    to_owners(accf.at[row], cb, row * NP + lax.rem(q, width(row)), t_b.at[row], s_cb.at[row], par)

            for row in range(level + 3, 4):
                @pl.when(same(row))
                def _(row=row):
                    minus(accf, row, x, mf[row, m])

            minus(accf, 4, x, mf[4, m])
            minus(accf, 5, x, mf[5, m])
            if level == 2:
                to_team(lambda k: accf.at[pl.ds(4, 2), k], r45.at[q], t_rows.at[0], s_rows.at[0])
        else:
            minus(accf, 4, x, mf[4, m])
            to_team(lambda k: accf.at[4, k], r4.at[q], t_rows.at[1], s_rows.at[1])
            minus(accf, 5, x, mf[5, m])
            to_team(lambda k: accf.at[5, k], r5.at[q], t_rows.at[2], s_rows.at[2])

        @pl.when(diag)
        def _():
            accb[level] = mm_t(x, uinv[level]).reshape(NS, 8, 128)

    def forward_own(level):
        n = width(level)
        wait_bytes(ca.at[pl.ds(level * NP, n)], s_ca.at[level])
        total = jnp.sum(ca[level * NP:level * NP + n], axis=0)
        if level >= 2:
            wait_bytes(cb.at[pl.ds(level * NP, n)], s_cb.at[level])
            total = total + jnp.sum(cb[level * NP:level * NP + n], axis=0)
        own[level] = total
        xf[level, slot] = total

        @pl.loop(1, NP)
        def _(d):
            push(own.at[level], xf.at[level, slot], t_ag.at[level], s_x.at[level], jnp.bitwise_xor(r, d), c, False)

    def prepare_back():
        for copy in copies[6:]:
            copy.wait()
        for m in range(3):
            for row in range(0, 2 * m + 1):
                mb[row, m] = fold(uinv[row], upp[row, m], upat[row, m])

    @pl.when(even)
    def _():
        forward_hold(0)
        give(5, 4, mf.at[5, 2])
        prepare_back()
        pl.when(owner)(functools.partial(forward_own, 2))
        forward_hold(2)
        give(3, 4, mb.at[3, 2])
        give(1, 2, mb.at[1, 1])
        give(0, 2, mb.at[0, 1])

    @pl.when(odd)
    def _():
        prepare_back()
        pl.when(owner)(functools.partial(forward_own, 1))
        forward_hold(1)
        give(4, 5, mb.at[4, 2])
        pl.when(owner)(functools.partial(forward_own, 3))
        forward_hold(3)
        give(2, 3, mb.at[2, 1])
        give(1, 3, mb.at[1, 1])
        give(0, 3, mb.at[0, 1])
        give(0, 1, mb.at[0, 0])

    def take(row, col):
        first, n = HELD[row, col]
        wait_bytes(held.at[pl.ds(first, n)], s_held.at[GROUP[row, col]])
        for i in range(first // 2, (first + n) // 2):
            high, low_ = split(jnp.concatenate([held[2 * i], held[2 * i + 1]], axis=1))
            wh[i] = high
            wl[i] = low_

    def apply(row, col, name):
        first, n = HELD[row, col]
        base, _ = GATHERED[name]
        total = jnp.zeros((8, 128), F32)
        for i in range(n // 2):
            high, low_ = split(jnp.concatenate([seen[base + 2 * i], seen[base + 2 * i + 1]], axis=1))
            both = dot_t(jnp.concatenate([high, low_], axis=0), wh[first // 2 + i])
            total = total + both[0:8] + both[8:16] + dot_t(high, wl[first // 2 + i])
        return total

    def gather(name, value):
        base, n = GATHERED[name]
        i = STEP[name]
        mine[i] = value
        place = base + lax.rem(r, n)
        seen[place] = value

        @pl.loop(1, n)
        def _(d):
            push(mine.at[i], seen.at[place], t_seen.at[i], s_seen.at[i], jnp.bitwise_xor(r, d), c, False)

    def gathered(name):
        base, n = GATHERED[name]
        wait_bytes(seen.at[pl.ds(base, n - 1)], s_seen.at[STEP[name]])

    def to_holders(level, name):
        @pl.loop(0, NP)
        def _(row):
            push(
                mine.at[STEP[name]], xb.at[level, k_me], t_z.at[level], s_z.at[level],
                row, (level % 2) * NP + r, True,
            )

    def deliver(level, source, n):
        @pl.loop(0, 2 * NP)
        def _(col):
            push(source, out.at[pl.ds(level, n), k_me], t_out.at[level], s_out, r, col, True)

    @pl.when(team)
    def _():
        wait_bytes(r45, s_rows.at[0])
        before = jnp.sum(r45[...], axis=0)
        wait_bytes(r4, s_rows.at[1])
        x4 = jnp.sum(r4[...], axis=0) + before[0]
        gather("x4", x4)
        take(5, 4)
        u4 = mm_t(x4, uinv[4])
        wait_bytes(r5, s_rows.at[2])
        z5 = jnp.sum(r5[...], axis=0) + before[1]
        gathered("x4")
        z5 = z5 - apply(5, 4, "x4")
        gather("z5", z5)
        to_holders(5, "z5")
        deliver(5, mine.at[pl.ds(STEP["z5"], 1)], 1)
        take(4, 5)
        gathered("z5")
        z4 = u4 - apply(4, 5, "z5")
        gather("z4", z4)
        to_holders(4, "z4")
        deliver(4, mine.at[pl.ds(STEP["z4"], 1)], 1)
        take(3, 4)

    @pl.when(odd)
    def _():
        wait_bytes(xb.at[5], s_z.at[5])
        z = xb[5].reshape(64, 128)
        minus(accb, 3, z, mb[3, 2])
        to_team(lambda k: accb.at[3, k], d3.at[q], t_rows.at[3], s_rows.at[3])
        for row in range(3):
            minus(accb, row, z, mb[row, 2])
        to_team(lambda k: accb.at[pl.ds(0, 3), k], d5.at[q], t_rows.at[4], s_rows.at[4])

    @pl.when(team)
    def _():
        wait_bytes(d3, s_rows.at[3])
        z3 = jnp.sum(d3[...], axis=0)
        gathered("z4")
        z3 = z3 - apply(3, 4, "z4")
        gather("z3", z3)
        deliver(3, mine.at[pl.ds(STEP["z3"], 1)], 1)

    @pl.when(even)
    def _():
        wait_bytes(xb.at[4], s_z.at[4])
        z = xb[4].reshape(64, 128)
        for row in range(3):
            minus(accb, row, z, mb[row, 2])
        to_team(lambda k: accb.at[pl.ds(0, 3), k], d4.at[q], t_rows.at[5], s_rows.at[5])

    @pl.when(team)
    def _():
        take(2, 3)
        take(1, 3)
        take(1, 2)
        wait_bytes(d5, s_rows.at[4])
        late = jnp.sum(d5[...], axis=0)
        gathered("z3")
        late2 = late[2] - apply(2, 3, "z3")
        late1 = late[1] - apply(1, 3, "z3")
        wait_bytes(d4, s_rows.at[5])
        last = jnp.sum(d4[...], axis=0)
        gather("z2", late2 + last[2])
        deliver(2, mine.at[pl.ds(STEP["z2"], 1)], 1)
        take(0, 3)
        take(0, 2)
        take(0, 1)
        late0 = late[0] + last[0] - apply(0, 3, "z3")
        gathered("z2")
        gather("z1", late1 + last[1] - apply(1, 2, "z2"))
        late0 = late0 - apply(0, 2, "z2")
        gathered("z1")
        mine[6] = late0 - apply(0, 1, "z1")
        mine[7] = mine[5]
        deliver(0, mine.at[pl.ds(6, 2)], 2)

    @pl.when(jnp.logical_and(diag, even))
    def _():
        @pl.loop(1, NP)
        def _(d):
            wait_bytes(xf.at[0], t_x0.at[d])

    def slices(n):
        return ca.at[pl.ds(0, n)]

    for level in range(3):
        row = level + 1

        @pl.when(jnp.logical_and(par == level % 2, same(row)))
        def _(row=row):
            wait_bytes(slices(NS), t_a.at[row])

        @pl.when(jnp.logical_and(par == row % 2, owner))
        def _(row=row):
            wait_bytes(slices(NP - 1), t_ag.at[row])

        if level + 2 < 4:
            @pl.when(jnp.logical_and(par == level % 2, same(level + 2)))
            def _(row=level + 2):
                @pl.when(diag)
                def _():
                    wait_bytes(slices(NS - 1), t_b.at[row])

                @pl.when(jnp.logical_not(diag))
                def _():
                    wait_bytes(slices(NS), t_b.at[row])

    def sent_rows(i, n):
        @pl.when(team)
        def _():
            wait_bytes(slices((NS - 1) * n), t_rows.at[i])

        @pl.when(jnp.logical_not(team))
        def _():
            wait_bytes(slices(NS * n), t_rows.at[i])

    def sent_blocks(row, col):
        @pl.when(same(col))
        def _():
            i = GROUP[row, col]

            @pl.when(team)
            def _():
                wait_bytes(held.at[pl.ds(0, NS - 1)], t_held.at[i])

            @pl.when(jnp.logical_not(team))
            def _():
                wait_bytes(held.at[pl.ds(0, NS)], t_held.at[i])

    @pl.when(even)
    def _():
        sent_rows(0, 2)
        sent_rows(5, 3)
        for key in ((5, 4), (3, 4), (1, 2), (0, 2)):
            sent_blocks(*key)

    @pl.when(odd)
    def _():
        sent_rows(1, 1)
        sent_rows(2, 1)
        sent_rows(3, 1)
        sent_rows(4, 3)
        for key in ((4, 5), (2, 3), (1, 3), (0, 3), (0, 1)):
            sent_blocks(*key)

    @pl.when(team)
    def _():
        for name, (_, n) in GATHERED.items():
            wait_bytes(slices(n - 1), t_seen.at[STEP[name]])
        for level in (5, 4):
            own_seat = jnp.logical_and(diag, par == level % 2)

            @pl.when(own_seat)
            def _(level=level):
                wait_bytes(slices(NP - 1), t_z.at[level])

            @pl.when(jnp.logical_not(own_seat))
            def _(level=level):
                wait_bytes(slices(NP), t_z.at[level])
        for level in (5, 4, 3, 2):
            wait_bytes(slices(2 * NP - 1), t_out.at[level])
        wait_bytes(slices(2 * (2 * NP - 1)), t_out.at[0])

    wait_bytes(out, s_out)


def shards(rhs, lower, lower_pattern, lower_inv, upper, upper_pattern, upper_inv):
    v = pltpu.VMEM
    dma = pltpu.SemaphoreType.DMA
    slices = (NL, NS, 8, 128)
    parts = (NL * NP, 8, 128)
    blocks = (NL, 3, 128, 128)
    got = pl.pallas_call(
        kernel,
        out_shape=jax.ShapeDtypeStruct(slices, F32),
        in_specs=[pl.BlockSpec(memory_space=pltpu.SMEM)] * 2 + [pl.BlockSpec(memory_space=pl.ANY)] * 5,
        out_specs=pl.BlockSpec(memory_space=pltpu.VMEM),
        scratch_shapes=[
            v((NL, 64, 128), F32), v(blocks, F32), v((NL, 128, 128), F32), v(blocks, F32), v((NL, 128, 128), F32),
            v(blocks, F32), v(blocks, F32), v(slices, F32), v(slices, F32), v(slices, F32), v(slices, F32),
            v(slices, F32), v(parts, F32), v(parts, F32), v((NL, 8, 128), F32),
            v((NHELD, 128, 128), F32), v((NHELD // 2, 128, 256), BF16), v((NHELD // 2, 128, 256), BF16),
            v((NGATHERED, 8, 128), F32), v((8, 8, 128), F32),
            v((NP, 8, 128), F32), v((NP, 8, 128), F32), v((NP, 2, 8, 128), F32),
            v((NP, 8, 128), F32), v((NP, 3, 8, 128), F32), v((NP, 3, 8, 128), F32),
            dma((9,)), dma((NL,)), dma((NL,)), dma((NL,)), dma((NL,)), dma((len(HELD),)), dma((len(GATHERED),)), dma((6,)), dma,
            dma((NP,)), dma((NL,)), dma((NL,)), dma((NL,)), dma((len(HELD),)), dma((len(GATHERED),)), dma((6,)),
            dma((NL,)), dma((NL,)),
        ],
        compiler_params=pltpu.CompilerParams(
            collective_id=0, has_side_effects=True, vmem_limit_bytes=60 * 1024 * 1024
        ),
        name="substitution",
    )(
        lower_pattern.reshape(NL, 3), upper_pattern.reshape(NL, 3), rhs.reshape(NL, 64, 128),
        lower.reshape(blocks), lower_inv.reshape(NL, 128, 128), upper.reshape(blocks), upper_inv.reshape(NL, 128, 128),
    )
    return got.reshape(NL, 1, 64, 128)


def solution(mesh):
    in_specs = (
        P(None, "prow", None, None),
        P(None, "prow", None, "pcol", None, None),
        P(None, "prow", None, "pcol"),
        P(None, "prow", None, None),
        P(None, "prow", None, "pcol", None, None),
        P(None, "prow", None, "pcol"),
        P(None, "prow", None, None),
    )
    out_specs = P(None, "prow", None, None)
    return jax.shard_map(shards, mesh=mesh, in_specs=in_specs, out_specs=out_specs, check_vma=False)
```

```python
import functools

import jax
import jax.numpy as jnp
from jax import lax
from jax.experimental import pallas as pl
from jax.experimental.pallas import tpu as pltpu
from jax.sharding import PartitionSpec as P

MESH = pl.DeviceIdType.MESH
NL = 6
NP = 16
NS = 8
NT = 4
TR = 16
BF16 = jnp.bfloat16
F32 = jnp.float32


def mm_t(x, w):
    return lax.dot_general(
        x, w, (((1,), (1,)), ((), ())),
        precision=lax.Precision.HIGHEST, preferred_element_type=F32,
    )


def mm(a, b):
    return lax.dot_general(
        a, b, (((1,), (0,)), ((), ())),
        precision=lax.Precision.HIGHEST, preferred_element_type=F32,
    )


HELD = {}
for _row, _col in ((5, 4), (4, 5), (3, 4), (2, 3), (1, 3), (0, 3), (1, 2), (0, 2), (0, 1)):
    HELD[_row, _col] = (sum(n for _, n in HELD.values()), min(NP, 1 << _col))
NHELD = sum(n for _, n in HELD.values())
GROUP = {key: i for i, key in enumerate(HELD)}
GATHERED = {"x4": (0, 16), "z5": (16, 16), "z4": (32, 16), "z3": (48, 8), "z2": (56, 4), "z1": (60, 2)}
STEP = {key: i for i, key in enumerate(GATHERED)}
NGATHERED = 62


def split(x):
    high = x.astype(BF16)
    return high, (x - high.astype(F32)).astype(BF16)


def dot_t(x, w):
    return lax.dot_general(x, w, (((1,), (1,)), ((), ())), preferred_element_type=F32)


def width(level):
    return min(NP, 1 << level)


def kernel(
    lpat, upat, rhs_h, low_h, linv_h, upp_h, uinv_h, out,
    rhs, low, linv, upp, uinv, mf, mb, accf, accb, xf, xb, pf, ca, cb, own,
    held, wh, wl, seen, mine, r4, r5, r45, d3, d5, d4,
    s_in, s_x, s_z, s_ca, s_cb, s_held, s_seen, s_rows, s_out,
    t_x0, t_a, t_b, t_ag, t_held, t_seen, t_rows, t_z, t_out,
):
    r = lax.axis_index("prow")
    c = lax.axis_index("pcol")
    par, q = c // NP, lax.rem(c, NP)
    even, odd = par == 0, par == 1
    dy = lax.rem(r // 2 - q // 2 + 9, 8)
    owner = dy < 4
    slot = jnp.where(owner, dy * 2 + lax.rem(r, 2), 0)
    diag = r == q

    def seat(k, row):
        return 8 * (2 * lax.rem(k, 2) + lax.rem(row, 2)) + 4 * (k // 2) + 2 * lax.rem(k, 2)

    col_x, col_z = c // 8, lax.rem(c, 8)
    half = col_x // 2
    turned = lax.rem(col_z + 8 - 2 * half, 8)
    team = jnp.logical_and(lax.rem(col_x, 2) == lax.rem(r, 2), lax.rem(turned, 4) == 0)
    k_me = jnp.where(team, half + 2 * (turned // 4), 0)

    def same(level):
        return r // width(level) == q // width(level)

    def near(position, j):
        return lax.rem(position // 2 + j // 2 + 7, 8) * 2 + lax.rem(j, 2)

    def at(row, col):
        return {"prow": row, "pcol": col}

    barrier = pltpu.get_barrier_semaphore()

    def tell(row, col):
        @pl.when(jnp.logical_not(jnp.logical_and(row == r, col == c)))
        def _():
            pl.semaphore_signal(barrier, inc=1, device_id=at(row, col), device_id_type=MESH)

    @pl.loop(0, NS)
    def _(j):
        tell(near(q, j), c)

    @pl.loop(0, NT)
    def _(k):
        tell(r, seat(k, r))
        tell(q, seat(k, q))

    @pl.when(owner)
    def _():
        @pl.loop(0, 2 * NP)
        def _(k):
            tell(q, k)

    @pl.when(team)
    def _():
        @pl.loop(0, 2 * NP)
        def _(k):
            tell(r, k)

        @pl.loop(0, NP)
        def _(k):
            tell(k, seat(k_me, k))

    loads = [(rhs_h, rhs), (linv_h, linv), (uinv_h, uinv)]
    for m in range(3):
        loads.append((low_h.at[pl.ds(2 * m + 1, 5 - 2 * m), m], low.at[pl.ds(2 * m + 1, 5 - 2 * m), m]))
    for m in range(3):
        loads.append((upp_h.at[pl.ds(0, 2 * m + 1), m], upp.at[pl.ds(0, 2 * m + 1), m]))
    copies = [pltpu.make_async_copy(a, b, s_in.at[i]) for i, (a, b) in enumerate(loads)]
    for copy in copies:
        copy.start()

    accf[...] = jnp.zeros_like(accf)
    accb[...] = jnp.zeros_like(accb)
    for copy in copies[:6]:
        copy.wait()

    top = mm(uinv[5], linv[5])

    def fold(inv, block, bit):
        return mm(inv, block * bit.astype(F32))

    for m in range(3):
        for row in range(2 * m + 1, NL):
            mf[row, m] = fold(top if row == 5 else linv[row], low[row, m], lpat[row, m])

    @pl.when(diag)
    def _():
        for row in range(1, NL):
            @pl.when(par == (row - 1) % 2)
            def _(row=row):
                accf[row] = mm_t(rhs[row], top if row == 5 else linv[row]).reshape(NS, 8, 128)

        @pl.when(even)
        def _():
            xf[0] = mm_t(rhs[0], linv[0]).reshape(NS, 8, 128)

    one = jnp.where(diag, 1, 0)
    sat = jnp.where(team, 1, 0)
    expected = 2 * NS - one + jnp.where(owner, NP - 1, 0) + NT - sat
    expected = expected + jnp.where(team, 2 * NP - 1 + NP - 1 + 2 * NP - one, 0)
    pl.semaphore_wait(barrier, expected)

    def wait_bytes(ref, sem):
        pltpu.make_async_copy(ref, ref, sem).wait()

    def push(source, target, send_sem, recv_sem, row, col, may_be_me):
        def remote():
            pltpu.make_async_remote_copy(
                source, target, send_sem, recv_sem, device_id=at(row, col), device_id_type=MESH
            ).start()

        if not may_be_me:
            remote()
            return
        me = jnp.logical_and(row == r, col == c)
        pl.when(jnp.logical_not(me))(remote)

        @pl.when(me)
        def _():
            pltpu.make_async_copy(source, target, recv_sem).start()

    @pl.when(jnp.logical_and(diag, even))
    def _():
        @pl.loop(1, NP)
        def _(d):
            push(xf.at[0], xf.at[0], t_x0.at[d], s_x.at[0], jnp.bitwise_xor(r, d), c, False)

    def to_owners(source, target, place, send_sem, recv_sem, parity):
        for j in range(NS):
            push(source.at[j], target.at[place], send_sem, recv_sem, near(r, j), parity * NP + r, parity is par)

    def to_team(piece, target, send_sem, recv_sem):
        for k in range(NT):
            push(piece(pl.ds(2 * k, 2)), target, send_sem, recv_sem, r, seat(k, r), True)

    def wait_slices(ref, sem):
        @pl.when(owner)
        def _():
            wait_bytes(ref.at[pl.ds(0, NS - 1)], sem)

        @pl.when(jnp.logical_not(owner))
        def _():
            wait_bytes(ref, sem)

    def give(row, col, source):
        first, n = HELD[row, col]
        i = GROUP[row, col]

        @pl.when(same(col))
        def _():
            @pl.loop(0, NT)
            def _(k):
                push(source, held.at[first + lax.rem(q, n)], t_held.at[i], s_held.at[i], r, seat(k, r), True)

    def minus(ref, row, x, w):
        ref[row] = ref[row] - mm_t(x, w).reshape(NS, 8, 128)

    def forward_hold(level):
        m = level // 2
        if level == 0:
            @pl.when(jnp.logical_not(diag))
            def _():
                wait_bytes(xf.at[0], s_x.at[0])
        else:
            wait_slices(xf.at[level], s_x.at[level])
        x = xf[level].reshape(64, 128)
        if level < 3:
            @pl.when(same(level + 1))
            def _():
                row = level + 1
                pf[level] = accf[row] - mm_t(x, mf[row, m]).reshape(NS, 8, 128)
                to_owners(pf.at[level], ca, row * NP + lax.rem(q, width(row)), t_a.at[row], s_ca.at[row], 1 - par)

            row = level + 2
            if row < 4:
                @pl.when(same(row))
                def _():
                    minus(accf, row, x, mf[row, m])
                    to_owners(accf.at[row], cb, row * NP + lax.rem(q, width(row)), t_b.at[row], s_cb.at[row], par)

            for row in range(level + 3, 4):
                @pl.when(same(row))
                def _(row=row):
                    minus(accf, row, x, mf[row, m])

            minus(accf, 4, x, mf[4, m])
            minus(accf, 5, x, mf[5, m])
            if level == 2:
                to_team(lambda k: accf.at[pl.ds(4, 2), k], r45.at[q], t_rows.at[0], s_rows.at[0])
        else:
            minus(accf, 4, x, mf[4, m])
            to_team(lambda k: accf.at[4, k], r4.at[q], t_rows.at[1], s_rows.at[1])
            minus(accf, 5, x, mf[5, m])
            to_team(lambda k: accf.at[5, k], r5.at[q], t_rows.at[2], s_rows.at[2])

        @pl.when(diag)
        def _():
            accb[level] = mm_t(x, uinv[level]).reshape(NS, 8, 128)

    def forward_own(level):
        n = width(level)
        wait_bytes(ca.at[pl.ds(level * NP, n)], s_ca.at[level])
        total = jnp.sum(ca[level * NP:level * NP + n], axis=0)
        if level >= 2:
            wait_bytes(cb.at[pl.ds(level * NP, n)], s_cb.at[level])
            total = total + jnp.sum(cb[level * NP:level * NP + n], axis=0)
        own[level] = total
        xf[level, slot] = total

        @pl.loop(1, NP)
        def _(d):
            push(own.at[level], xf.at[level, slot], t_ag.at[level], s_x.at[level], jnp.bitwise_xor(r, d), c, False)

    def prepare_back():
        for copy in copies[6:]:
            copy.wait()
        for m in range(3):
            for row in range(0, 2 * m + 1):
                mb[row, m] = fold(uinv[row], upp[row, m], upat[row, m])

    @pl.when(even)
    def _():
        forward_hold(0)
        give(5, 4, mf.at[5, 2])
        prepare_back()
        pl.when(owner)(functools.partial(forward_own, 2))
        forward_hold(2)
        give(3, 4, mb.at[3, 2])
        give(1, 2, mb.at[1, 1])
        give(0, 2, mb.at[0, 1])

    @pl.when(odd)
    def _():
        prepare_back()
        pl.when(owner)(functools.partial(forward_own, 1))
        forward_hold(1)
        give(4, 5, mb.at[4, 2])
        pl.when(owner)(functools.partial(forward_own, 3))
        forward_hold(3)
        give(2, 3, mb.at[2, 1])
        give(1, 3, mb.at[1, 1])
        give(0, 3, mb.at[0, 1])
        give(0, 1, mb.at[0, 0])

    def take(row, col):
        first, n = HELD[row, col]
        wait_bytes(held.at[pl.ds(first, n)], s_held.at[GROUP[row, col]])
        for i in range(first // 2, (first + n) // 2):
            high, low_ = split(jnp.concatenate([held[2 * i], held[2 * i + 1]], axis=1))
            wh[i] = high
            wl[i] = low_

    def apply(row, col, name):
        first, n = HELD[row, col]
        base, _ = GATHERED[name]
        total = jnp.zeros((TR, 128), F32)
        for i in range(n // 2):
            high, low_ = split(jnp.concatenate(
                [seen[base + 2 * i].reshape(TR, 128), seen[base + 2 * i + 1].reshape(TR, 128)], axis=1
            ))
            both = dot_t(jnp.concatenate([high, low_], axis=0), wh[first // 2 + i])
            total = total + both[0:TR] + both[TR:2 * TR] + dot_t(high, wl[first // 2 + i])
        return total

    def gather(name, value):
        base, n = GATHERED[name]
        i = STEP[name]
        mine[i] = value.reshape(2, 8, 128)
        place = base + lax.rem(r, n)
        seen[place] = value.reshape(2, 8, 128)

        @pl.loop(1, n)
        def _(d):
            row = jnp.bitwise_xor(r, d)
            push(mine.at[i], seen.at[place], t_seen.at[i], s_seen.at[i], row, seat(k_me, row), False)

    def gathered(name):
        base, n = GATHERED[name]
        wait_bytes(seen.at[pl.ds(base, n - 1)], s_seen.at[STEP[name]])

    def to_holders(level, name):
        @pl.loop(0, NP)
        def _(row):
            push(
                mine.at[STEP[name]], xb.at[level, pl.ds(2 * k_me, 2)], t_z.at[level], s_z.at[level],
                row, (level % 2) * NP + r, True,
            )

    def deliver(level, source, n):
        @pl.loop(0, 2 * NP)
        def _(col):
            push(source, out.at[pl.ds(level, n), pl.ds(2 * k_me, 2)], t_out.at[level], s_out, r, col, True)

    @pl.when(team)
    def _():
        wait_bytes(r45, s_rows.at[0])
        before = jnp.sum(r45[...], axis=0).reshape(2, TR, 128)
        wait_bytes(r4, s_rows.at[1])
        x4 = jnp.sum(r4[...], axis=0).reshape(TR, 128) + before[0]
        gather("x4", x4)
        take(5, 4)
        u4 = mm_t(x4, uinv[4])
        wait_bytes(r5, s_rows.at[2])
        z5 = jnp.sum(r5[...], axis=0).reshape(TR, 128) + before[1]
        gathered("x4")
        z5 = z5 - apply(5, 4, "x4")
        gather("z5", z5)
        to_holders(5, "z5")
        deliver(5, mine.at[pl.ds(STEP["z5"], 1)], 1)
        take(4, 5)
        gathered("z5")
        z4 = u4 - apply(4, 5, "z5")
        gather("z4", z4)
        to_holders(4, "z4")
        deliver(4, mine.at[pl.ds(STEP["z4"], 1)], 1)
        take(3, 4)

    @pl.when(odd)
    def _():
        wait_bytes(xb.at[5], s_z.at[5])
        z = xb[5].reshape(64, 128)
        minus(accb, 3, z, mb[3, 2])
        to_team(lambda k: accb.at[3, k], d3.at[q], t_rows.at[3], s_rows.at[3])
        for row in range(3):
            minus(accb, row, z, mb[row, 2])
        to_team(lambda k: accb.at[pl.ds(0, 3), k], d5.at[q], t_rows.at[4], s_rows.at[4])

    @pl.when(team)
    def _():
        wait_bytes(d3, s_rows.at[3])
        z3 = jnp.sum(d3[...], axis=0).reshape(TR, 128)
        gathered("z4")
        z3 = z3 - apply(3, 4, "z4")
        gather("z3", z3)
        deliver(3, mine.at[pl.ds(STEP["z3"], 1)], 1)

    @pl.when(even)
    def _():
        wait_bytes(xb.at[4], s_z.at[4])
        z = xb[4].reshape(64, 128)
        for row in range(3):
            minus(accb, row, z, mb[row, 2])
        to_team(lambda k: accb.at[pl.ds(0, 3), k], d4.at[q], t_rows.at[5], s_rows.at[5])

    @pl.when(team)
    def _():
        take(2, 3)
        take(1, 3)
        take(1, 2)
        wait_bytes(d5, s_rows.at[4])
        late = jnp.sum(d5[...], axis=0).reshape(3, TR, 128)
        gathered("z3")
        late2 = late[2] - apply(2, 3, "z3")
        late1 = late[1] - apply(1, 3, "z3")
        wait_bytes(d4, s_rows.at[5])
        last = jnp.sum(d4[...], axis=0).reshape(3, TR, 128)
        gather("z2", late2 + last[2])
        deliver(2, mine.at[pl.ds(STEP["z2"], 1)], 1)
        take(0, 3)
        take(0, 2)
        take(0, 1)
        late0 = late[0] + last[0] - apply(0, 3, "z3")
        gathered("z2")
        gather("z1", late1 + last[1] - apply(1, 2, "z2"))
        late0 = late0 - apply(0, 2, "z2")
        gathered("z1")
        mine[6] = (late0 - apply(0, 1, "z1")).reshape(2, 8, 128)
        mine[7] = mine[5]
        deliver(0, mine.at[pl.ds(6, 2)], 2)

    @pl.when(jnp.logical_and(diag, even))
    def _():
        @pl.loop(1, NP)
        def _(d):
            wait_bytes(xf.at[0], t_x0.at[d])

    def slices(n):
        return ca.at[pl.ds(0, n)]

    for level in range(3):
        row = level + 1

        @pl.when(jnp.logical_and(par == level % 2, same(row)))
        def _(row=row):
            wait_bytes(slices(NS), t_a.at[row])

        @pl.when(jnp.logical_and(par == row % 2, owner))
        def _(row=row):
            wait_bytes(slices(NP - 1), t_ag.at[row])

        if level + 2 < 4:
            @pl.when(jnp.logical_and(par == level % 2, same(level + 2)))
            def _(row=level + 2):
                @pl.when(diag)
                def _():
                    wait_bytes(slices(NS - 1), t_b.at[row])

                @pl.when(jnp.logical_not(diag))
                def _():
                    wait_bytes(slices(NS), t_b.at[row])

    def sent_rows(i, n):
        @pl.when(team)
        def _():
            wait_bytes(slices(2 * (NT - 1) * n), t_rows.at[i])

        @pl.when(jnp.logical_not(team))
        def _():
            wait_bytes(slices(2 * NT * n), t_rows.at[i])

    def sent_blocks(row, col):
        @pl.when(same(col))
        def _():
            i = GROUP[row, col]

            @pl.when(team)
            def _():
                wait_bytes(held.at[pl.ds(0, NT - 1)], t_held.at[i])

            @pl.when(jnp.logical_not(team))
            def _():
                wait_bytes(held.at[pl.ds(0, NT)], t_held.at[i])

    @pl.when(even)
    def _():
        sent_rows(0, 2)
        sent_rows(5, 3)
        for key in ((5, 4), (3, 4), (1, 2), (0, 2)):
            sent_blocks(*key)

    @pl.when(odd)
    def _():
        sent_rows(1, 1)
        sent_rows(2, 1)
        sent_rows(3, 1)
        sent_rows(4, 3)
        for key in ((4, 5), (2, 3), (1, 3), (0, 3), (0, 1)):
            sent_blocks(*key)

    @pl.when(team)
    def _():
        for name, (_, n) in GATHERED.items():
            wait_bytes(slices(2 * (n - 1)), t_seen.at[STEP[name]])
        for level in (5, 4):
            own_seat = jnp.logical_and(diag, par == level % 2)

            @pl.when(own_seat)
            def _(level=level):
                wait_bytes(slices(2 * (NP - 1)), t_z.at[level])

            @pl.when(jnp.logical_not(own_seat))
            def _(level=level):
                wait_bytes(slices(2 * NP), t_z.at[level])
        for level in (5, 4, 3, 2):
            wait_bytes(slices(2 * (2 * NP - 1)), t_out.at[level])
        wait_bytes(seen, t_out.at[0])

    wait_bytes(out, s_out)


def shards(rhs, lower, lower_pattern, lower_inv, upper, upper_pattern, upper_inv):
    v = pltpu.VMEM
    dma = pltpu.SemaphoreType.DMA
    slices = (NL, NS, 8, 128)
    parts = (NL * NP, 8, 128)
    blocks = (NL, 3, 128, 128)
    got = pl.pallas_call(
        kernel,
        out_shape=jax.ShapeDtypeStruct(slices, F32),
        in_specs=[pl.BlockSpec(memory_space=pltpu.SMEM)] * 2 + [pl.BlockSpec(memory_space=pl.ANY)] * 5,
        out_specs=pl.BlockSpec(memory_space=pltpu.VMEM),
        scratch_shapes=[
            v((NL, 64, 128), F32), v(blocks, F32), v((NL, 128, 128), F32), v(blocks, F32), v((NL, 128, 128), F32),
            v(blocks, F32), v(blocks, F32), v(slices, F32), v(slices, F32), v(slices, F32), v(slices, F32),
            v(slices, F32), v(parts, F32), v(parts, F32), v((NL, 8, 128), F32),
            v((NHELD, 128, 128), F32), v((NHELD // 2, 128, 256), BF16), v((NHELD // 2, 128, 256), BF16),
            v((NGATHERED, 2, 8, 128), F32), v((8, 2, 8, 128), F32),
            v((NP, 2, 8, 128), F32), v((NP, 2, 8, 128), F32), v((NP, 2, 2, 8, 128), F32),
            v((NP, 2, 8, 128), F32), v((NP, 3, 2, 8, 128), F32), v((NP, 3, 2, 8, 128), F32),
            dma((9,)), dma((NL,)), dma((NL,)), dma((NL,)), dma((NL,)), dma((len(HELD),)), dma((len(GATHERED),)), dma((6,)), dma,
            dma((NP,)), dma((NL,)), dma((NL,)), dma((NL,)), dma((len(HELD),)), dma((len(GATHERED),)), dma((6,)),
            dma((NL,)), dma((NL,)),
        ],
        compiler_params=pltpu.CompilerParams(
            collective_id=0, has_side_effects=True, vmem_limit_bytes=60 * 1024 * 1024
        ),
        name="substitution",
    )(
        lower_pattern.reshape(NL, 3), upper_pattern.reshape(NL, 3), rhs.reshape(NL, 64, 128),
        lower.reshape(blocks), lower_inv.reshape(NL, 128, 128), upper.reshape(blocks), upper_inv.reshape(NL, 128, 128),
    )
    return got.reshape(NL, 1, 64, 128)


def solution(mesh):
    in_specs = (
        P(None, "prow", None, None),
        P(None, "prow", None, "pcol", None, None),
        P(None, "prow", None, "pcol"),
        P(None, "prow", None, None),
        P(None, "prow", None, "pcol", None, None),
        P(None, "prow", None, "pcol"),
        P(None, "prow", None, None),
    )
    out_specs = P(None, "prow", None, None)
    return jax.shard_map(shards, mesh=mesh, in_specs=in_specs, out_specs=out_specs, check_vma=False)
```

```python
import functools

import jax
import jax.numpy as jnp
from jax import lax
from jax.experimental import pallas as pl
from jax.experimental.pallas import tpu as pltpu
from jax.sharding import PartitionSpec as P

MESH = pl.DeviceIdType.MESH
NL = 6
NP = 16
NS = 8
NT = 4
TR = 16
BF16 = jnp.bfloat16
F32 = jnp.float32


def mm_t(x, w):
    return lax.dot_general(
        x, w, (((1,), (1,)), ((), ())),
        precision=lax.Precision.HIGHEST, preferred_element_type=F32,
    )


def mm(a, b):
    return lax.dot_general(
        a, b, (((1,), (0,)), ((), ())),
        precision=lax.Precision.HIGHEST, preferred_element_type=F32,
    )


HELD = {}
for _row, _col in ((5, 4), (4, 5), (3, 4), (2, 3), (1, 3), (0, 3), (1, 2), (0, 2), (0, 1)):
    HELD[_row, _col] = (sum(n for _, n in HELD.values()), min(NP, 1 << _col))
NHELD = sum(n for _, n in HELD.values())
GROUP = {key: i for i, key in enumerate(HELD)}
GATHERED = {"x4": (0, 16), "z5": (16, 16), "z4": (32, 16), "z3": (48, 8), "z2": (56, 4), "z1": (60, 2)}
STEP = {key: i for i, key in enumerate(GATHERED)}
NGATHERED = 62


def split(x):
    high = x.astype(BF16)
    return high, (x - high.astype(F32)).astype(BF16)


def dot_t(x, w):
    return lax.dot_general(x, w, (((1,), (1,)), ((), ())), preferred_element_type=F32)


def width(level):
    return min(NP, 1 << level)


def kernel(
    lpat, upat, rhs_h, low_h, linv_h, upp_h, uinv_h, out,
    rhs, low, linv, upp, uinv, mf, mb, accf, accb, xf, xb, pf, ca, cb, own,
    e1, held, wh, wl, seen, mine, r4, r5, r45, d3, d5, d4,
    s_in, s_x, s_z, s_ca, s_cb, s_held, s_seen, s_rows, s_out, s_e1, t_e1,
    t_x0, t_a, t_b, t_ag, t_held, t_seen, t_rows, t_z, t_out,
):
    r = lax.axis_index("prow")
    c = lax.axis_index("pcol")
    par, q = c // NP, lax.rem(c, NP)
    even, odd = par == 0, par == 1
    dy = lax.rem(r // 2 - q // 2 + 9, 8)
    owner = dy < 4
    slot = jnp.where(owner, dy * 2 + lax.rem(r, 2), 0)
    diag = r == q

    def seat(k, row):
        return 8 * (2 * lax.rem(k, 2) + lax.rem(row, 2)) + 4 * (k // 2) + 2 * lax.rem(k, 2)

    col_x, col_z = c // 8, lax.rem(c, 8)
    half = col_x // 2
    turned = lax.rem(col_z + 8 - 2 * half, 8)
    team = jnp.logical_and(lax.rem(col_x, 2) == lax.rem(r, 2), lax.rem(turned, 4) == 0)
    k_me = jnp.where(team, half + 2 * (turned // 4), 0)

    def same(level):
        return r // width(level) == q // width(level)

    def near(position, j):
        return lax.rem(position // 2 + j // 2 + 7, 8) * 2 + lax.rem(j, 2)

    def at(row, col):
        return {"prow": row, "pcol": col}

    barrier = pltpu.get_barrier_semaphore()

    def tell(row, col):
        @pl.when(jnp.logical_not(jnp.logical_and(row == r, col == c)))
        def _():
            pl.semaphore_signal(barrier, inc=1, device_id=at(row, col), device_id_type=MESH)

    @pl.loop(0, NS)
    def _(j):
        tell(near(q, j), c)

    @pl.loop(0, NT)
    def _(k):
        tell(r, seat(k, r))
        tell(q, seat(k, q))

    @pl.when(owner)
    def _():
        @pl.loop(0, 2 * NP)
        def _(k):
            tell(q, k)

    @pl.when(team)
    def _():
        @pl.loop(0, 2 * NP)
        def _(k):
            tell(r, k)

        @pl.loop(0, NP)
        def _(k):
            tell(k, seat(k_me, k))

    loads = [(rhs_h, rhs), (linv_h, linv), (uinv_h, uinv)]
    for m in range(3):
        loads.append((low_h.at[pl.ds(2 * m + 1, 5 - 2 * m), m], low.at[pl.ds(2 * m + 1, 5 - 2 * m), m]))
    for m in range(3):
        loads.append((upp_h.at[pl.ds(0, 2 * m + 1), m], upp.at[pl.ds(0, 2 * m + 1), m]))
    copies = [pltpu.make_async_copy(a, b, s_in.at[i]) for i, (a, b) in enumerate(loads)]
    for copy in copies:
        copy.start()

    accf[...] = jnp.zeros_like(accf)
    accb[...] = jnp.zeros_like(accb)
    for copy in copies[:6]:
        copy.wait()

    top = mm(uinv[5], linv[5])

    def fold(inv, block, bit):
        return mm(inv, block * bit.astype(F32))

    for m in range(3):
        for row in range(2 * m + 1, NL):
            mf[row, m] = fold(top if row == 5 else linv[row], low[row, m], lpat[m, 0, row])

    @pl.when(diag)
    def _():
        for row in range(1, NL):
            @pl.when(par == (row - 1) % 2)
            def _(row=row):
                accf[row] = mm_t(rhs[row], top if row == 5 else linv[row]).reshape(NS, 8, 128)

        @pl.when(even)
        def _():
            xf[0] = mm_t(rhs[0], linv[0]).reshape(NS, 8, 128)

    one = jnp.where(diag, 1, 0)
    sat = jnp.where(team, 1, 0)
    expected = 2 * NS - one + jnp.where(owner, NP - 1, 0) + NT - sat
    expected = expected + jnp.where(team, 2 * NP - 1 + NP - 1 + 2 * NP - one, 0)
    pl.semaphore_wait(barrier, expected)

    def wait_bytes(ref, sem):
        pltpu.make_async_copy(ref, ref, sem).wait()

    def push(source, target, send_sem, recv_sem, row, col, may_be_me):
        def remote():
            pltpu.make_async_remote_copy(
                source, target, send_sem, recv_sem, device_id=at(row, col), device_id_type=MESH
            ).start()

        if not may_be_me:
            remote()
            return
        me = jnp.logical_and(row == r, col == c)
        pl.when(jnp.logical_not(me))(remote)

        @pl.when(me)
        def _():
            pltpu.make_async_copy(source, target, recv_sem).start()

    @pl.when(jnp.logical_and(diag, even))
    def _():
        @pl.loop(1, NP)
        def _(d):
            push(xf.at[0], xf.at[0], t_x0.at[d], s_x.at[0], jnp.bitwise_xor(r, d), c, False)

    def to_owners(source, target, place, send_sem, recv_sem, parity):
        for j in (6, 7, 0, 1, 4, 5, 2, 3):
            push(source.at[j], target.at[place], send_sem, recv_sem, near(r, j), parity * NP + r, parity is par)

    def to_team(piece, target, send_sem, recv_sem):
        for k in range(NT):
            push(piece(pl.ds(2 * k, 2)), target, send_sem, recv_sem, r, seat(k, r), True)

    def wait_slices(ref, sem):
        @pl.when(owner)
        def _():
            wait_bytes(ref.at[pl.ds(0, NS - 1)], sem)

        @pl.when(jnp.logical_not(owner))
        def _():
            wait_bytes(ref, sem)

    def give(row, col, source):
        first, n = HELD[row, col]
        i = GROUP[row, col]

        @pl.when(same(col))
        def _():
            @pl.loop(0, NT)
            def _(k):
                push(source, held.at[first + lax.rem(q, n)], t_held.at[i], s_held.at[i], r, seat(k, r), True)

    def minus(ref, row, x, w):
        ref[row] = ref[row] - mm_t(x, w).reshape(NS, 8, 128)

    def forward_hold(level):
        m = level // 2
        if level == 0:
            @pl.when(jnp.logical_not(diag))
            def _():
                wait_bytes(xf.at[0], s_x.at[0])
        elif level == 1:
            @pl.when(same(2))
            def _():
                wait_bytes(e1, s_e1)
                xf[1] = e1[0] + e1[1]

            @pl.when(jnp.logical_not(same(2)))
            def _():
                wait_slices(xf.at[level], s_x.at[level])
        else:
            wait_slices(xf.at[level], s_x.at[level])
        x = xf[level].reshape(64, 128)
        if level < 3:
            @pl.when(same(level + 1))
            def _():
                row = level + 1
                pf[level] = accf[row] - mm_t(x, mf[row, m]).reshape(NS, 8, 128)
                if level == 0:
                    for d in range(4):
                        push(
                            pf.at[0], e1.at[lax.rem(q, 2)], t_e1, s_e1,
                            jnp.bitwise_xor(r, d), NP + r, False,
                        )
                to_owners(pf.at[level], ca, row * NP + lax.rem(q, width(row)), t_a.at[row], s_ca.at[row], 1 - par)

            row = level + 2
            if row < 4:
                @pl.when(same(row))
                def _():
                    minus(accf, row, x, mf[row, m])
                    to_owners(accf.at[row], cb, row * NP + lax.rem(q, width(row)), t_b.at[row], s_cb.at[row], par)

            for row in range(level + 3, 4):
                @pl.when(same(row))
                def _(row=row):
                    minus(accf, row, x, mf[row, m])

            minus(accf, 4, x, mf[4, m])
            minus(accf, 5, x, mf[5, m])
            if level == 2:
                to_team(lambda k: accf.at[pl.ds(4, 2), k], r45.at[q], t_rows.at[0], s_rows.at[0])
        else:
            minus(accf, 4, x, mf[4, m])
            to_team(lambda k: accf.at[4, k], r4.at[q], t_rows.at[1], s_rows.at[1])
            minus(accf, 5, x, mf[5, m])
            to_team(lambda k: accf.at[5, k], r5.at[q], t_rows.at[2], s_rows.at[2])

        @pl.when(diag)
        def _():
            accb[level] = mm_t(x, uinv[level]).reshape(NS, 8, 128)

    def forward_own(level):
        n = width(level)
        wait_bytes(ca.at[pl.ds(level * NP, n)], s_ca.at[level])
        total = jnp.sum(ca[level * NP:level * NP + n], axis=0)
        if level >= 2:
            wait_bytes(cb.at[pl.ds(level * NP, n)], s_cb.at[level])
            total = total + jnp.sum(cb[level * NP:level * NP + n], axis=0)
        own[level] = total
        if level > 1:
            xf[level, slot] = total

            @pl.loop(1, NP)
            def _(d):
                row = jnp.bitwise_xor(r, NP - d)
                push(own.at[level], xf.at[level, slot], t_ag.at[level], s_x.at[level], row, c, False)
        else:
            @pl.when(jnp.logical_not(same(2)))
            def _():
                xf[level, slot] = total

            @pl.loop(0, NP)
            def _(d):
                row = jnp.bitwise_xor(r, d)

                @pl.when(jnp.logical_and(row // 4 != q // 4, row != r))
                def _():
                    push(own.at[level], xf.at[level, slot], t_ag.at[level], s_x.at[level], row, c, False)

    def prepare_back():
        for copy in copies[6:]:
            copy.wait()
        for m in range(3):
            for row in range(0, 2 * m + 1):
                mb[row, m] = fold(uinv[row], upp[row, m], upat[m, 0, row])

    @pl.when(even)
    def _():
        forward_hold(0)
        give(5, 4, mf.at[5, 2])
        prepare_back()
        pl.when(owner)(functools.partial(forward_own, 2))
        forward_hold(2)
        give(3, 4, mb.at[3, 2])
        give(1, 2, mb.at[1, 1])
        give(0, 2, mb.at[0, 1])

    @pl.when(odd)
    def _():
        prepare_back()
        give(4, 5, mb.at[4, 2])
        pl.when(jnp.logical_and(owner, jnp.logical_not(same(2))))(functools.partial(forward_own, 1))
        forward_hold(1)
        pl.when(jnp.logical_and(owner, same(2)))(functools.partial(forward_own, 1))
        give(2, 3, mb.at[2, 1])
        give(1, 3, mb.at[1, 1])
        pl.when(owner)(functools.partial(forward_own, 3))
        forward_hold(3)
        give(0, 3, mb.at[0, 1])
        give(0, 1, mb.at[0, 0])

    def take(row, col):
        first, n = HELD[row, col]
        wait_bytes(held.at[pl.ds(first, n)], s_held.at[GROUP[row, col]])
        for i in range(first // 2, (first + n) // 2):
            high, low_ = split(jnp.concatenate([held[2 * i], held[2 * i + 1]], axis=1))
            wh[i] = high
            wl[i] = low_

    def apply(row, col, name):
        first, n = HELD[row, col]
        base, _ = GATHERED[name]
        total = jnp.zeros((TR, 128), F32)
        for i in range(n // 2):
            high, low_ = split(jnp.concatenate(
                [seen[base + 2 * i].reshape(TR, 128), seen[base + 2 * i + 1].reshape(TR, 128)], axis=1
            ))
            both = dot_t(jnp.concatenate([high, low_], axis=0), wh[first // 2 + i])
            total = total + both[0:TR] + both[TR:2 * TR] + dot_t(high, wl[first // 2 + i])
        return total

    def gather(name, value):
        base, n = GATHERED[name]
        i = STEP[name]
        mine[i] = value.reshape(2, 8, 128)
        place = base + lax.rem(r, n)
        seen[place] = value.reshape(2, 8, 128)

        @pl.loop(1, n)
        def _(d):
            row = jnp.bitwise_xor(r, n - d)
            push(mine.at[i], seen.at[place], t_seen.at[i], s_seen.at[i], row, seat(k_me, row), False)

    def gathered(name):
        base, n = GATHERED[name]
        wait_bytes(seen.at[pl.ds(base, n - 1)], s_seen.at[STEP[name]])

    def to_holders(level, name):
        @pl.loop(0, NP)
        def _(d):
            row = jnp.bitwise_xor(r, NP - 1 - d)
            push(
                mine.at[STEP[name]], xb.at[level, pl.ds(2 * k_me, 2)], t_z.at[level], s_z.at[level],
                row, (level % 2) * NP + r, True,
            )

    def deliver(level, source, n):
        @pl.loop(0, 2 * NP)
        def _(col):
            push(source, out.at[pl.ds(level, n), pl.ds(2 * k_me, 2)], t_out.at[level], s_out, r, col, True)

    @pl.when(team)
    def _():
        wait_bytes(r45, s_rows.at[0])
        before = jnp.sum(r45[...], axis=0).reshape(2, TR, 128)
        wait_bytes(r4, s_rows.at[1])
        x4 = jnp.sum(r4[...], axis=0).reshape(TR, 128) + before[0]
        gather("x4", x4)
        take(5, 4)
        u4 = mm_t(x4, uinv[4])
        wait_bytes(r5, s_rows.at[2])
        z5 = jnp.sum(r5[...], axis=0).reshape(TR, 128) + before[1]
        gathered("x4")
        z5 = z5 - apply(5, 4, "x4")
        gather("z5", z5)
        to_holders(5, "z5")
        deliver(5, mine.at[pl.ds(STEP["z5"], 1)], 1)
        take(4, 5)
        gathered("z5")
        z4 = u4 - apply(4, 5, "z5")
        gather("z4", z4)
        to_holders(4, "z4")
        deliver(4, mine.at[pl.ds(STEP["z4"], 1)], 1)
        take(3, 4)

    @pl.when(odd)
    def _():
        wait_bytes(xb.at[5], s_z.at[5])
        z = xb[5].reshape(64, 128)
        minus(accb, 3, z, mb[3, 2])
        to_team(lambda k: accb.at[3, k], d3.at[q], t_rows.at[3], s_rows.at[3])
        for row in range(3):
            minus(accb, row, z, mb[row, 2])
        to_team(lambda k: accb.at[pl.ds(0, 3), k], d5.at[q], t_rows.at[4], s_rows.at[4])

    @pl.when(team)
    def _():
        wait_bytes(d3, s_rows.at[3])
        z3 = jnp.sum(d3[...], axis=0).reshape(TR, 128)
        gathered("z4")
        z3 = z3 - apply(3, 4, "z4")
        gather("z3", z3)
        deliver(3, mine.at[pl.ds(STEP["z3"], 1)], 1)

    @pl.when(even)
    def _():
        wait_bytes(xb.at[4], s_z.at[4])
        z = xb[4].reshape(64, 128)
        for row in range(3):
            minus(accb, row, z, mb[row, 2])
        to_team(lambda k: accb.at[pl.ds(0, 3), k], d4.at[q], t_rows.at[5], s_rows.at[5])

    @pl.when(team)
    def _():
        take(2, 3)
        take(1, 3)
        take(1, 2)
        wait_bytes(d5, s_rows.at[4])
        late = jnp.sum(d5[...], axis=0).reshape(3, TR, 128)
        gathered("z3")
        late2 = late[2] - apply(2, 3, "z3")
        late1 = late[1] - apply(1, 3, "z3")
        wait_bytes(d4, s_rows.at[5])
        last = jnp.sum(d4[...], axis=0).reshape(3, TR, 128)
        gather("z2", late2 + last[2])
        deliver(2, mine.at[pl.ds(STEP["z2"], 1)], 1)
        take(0, 3)
        take(0, 2)
        take(0, 1)
        late0 = late[0] + last[0] - apply(0, 3, "z3")
        gathered("z2")
        gather("z1", late1 + last[1] - apply(1, 2, "z2"))
        late0 = late0 - apply(0, 2, "z2")
        deliver(1, mine.at[pl.ds(STEP["z1"], 1)], 1)
        gathered("z1")
        mine[6] = (late0 - apply(0, 1, "z1")).reshape(2, 8, 128)
        deliver(0, mine.at[pl.ds(6, 1)], 1)

    @pl.when(jnp.logical_and(diag, even))
    def _():
        @pl.loop(1, NP)
        def _(d):
            wait_bytes(xf.at[0], t_x0.at[d])

    def slices(n):
        return ca.at[pl.ds(0, n)]

    for level in range(3):
        row = level + 1

        @pl.when(jnp.logical_and(par == level % 2, same(row)))
        def _(row=row):
            wait_bytes(slices(NS), t_a.at[row])
            if row == 1:
                wait_bytes(xf.at[pl.ds(0, 4)], t_e1)

        @pl.when(jnp.logical_and(par == row % 2, owner))
        def _(row=row):
            if row > 1:
                wait_bytes(slices(NP - 1), t_ag.at[row])
                return

            @pl.when(same(2))
            def _():
                wait_bytes(slices(NP - 4), t_ag.at[row])

            @pl.when(jnp.logical_not(same(2)))
            def _():
                wait_bytes(slices(NP - 5), t_ag.at[row])

        if level + 2 < 4:
            @pl.when(jnp.logical_and(par == level % 2, same(level + 2)))
            def _(row=level + 2):
                @pl.when(diag)
                def _():
                    wait_bytes(slices(NS - 1), t_b.at[row])

                @pl.when(jnp.logical_not(diag))
                def _():
                    wait_bytes(slices(NS), t_b.at[row])

    def sent_rows(i, n):
        @pl.when(team)
        def _():
            wait_bytes(slices(2 * (NT - 1) * n), t_rows.at[i])

        @pl.when(jnp.logical_not(team))
        def _():
            wait_bytes(slices(2 * NT * n), t_rows.at[i])

    def sent_blocks(row, col):
        @pl.when(same(col))
        def _():
            i = GROUP[row, col]

            @pl.when(team)
            def _():
                wait_bytes(held.at[pl.ds(0, NT - 1)], t_held.at[i])

            @pl.when(jnp.logical_not(team))
            def _():
                wait_bytes(held.at[pl.ds(0, NT)], t_held.at[i])

    @pl.when(even)
    def _():
        sent_rows(0, 2)
        sent_rows(5, 3)
        for key in ((5, 4), (3, 4), (1, 2), (0, 2)):
            sent_blocks(*key)

    @pl.when(odd)
    def _():
        sent_rows(1, 1)
        sent_rows(2, 1)
        sent_rows(3, 1)
        sent_rows(4, 3)
        for key in ((4, 5), (2, 3), (1, 3), (0, 3), (0, 1)):
            sent_blocks(*key)

    @pl.when(team)
    def _():
        for name, (_, n) in GATHERED.items():
            wait_bytes(slices(2 * (n - 1)), t_seen.at[STEP[name]])
        for level in (5, 4):
            own_seat = jnp.logical_and(diag, par == level % 2)

            @pl.when(own_seat)
            def _(level=level):
                wait_bytes(slices(2 * (NP - 1)), t_z.at[level])

            @pl.when(jnp.logical_not(own_seat))
            def _(level=level):
                wait_bytes(slices(2 * NP), t_z.at[level])
        for level in range(NL):
            wait_bytes(slices(2 * (2 * NP - 1)), t_out.at[level])

    wait_bytes(out, s_out)


def shards(rhs, lower, lower_pattern, lower_inv, upper, upper_pattern, upper_inv):
    v = pltpu.VMEM
    dma = pltpu.SemaphoreType.DMA
    slices = (NL, NS, 8, 128)
    parts = (NL * NP, 8, 128)
    blocks = (NL, 3, 128, 128)
    got = pl.pallas_call(
        kernel,
        out_shape=jax.ShapeDtypeStruct(slices, F32),
        in_specs=[pl.BlockSpec(memory_space=pltpu.SMEM)] * 2 + [pl.BlockSpec(memory_space=pl.ANY)] * 5,
        out_specs=pl.BlockSpec(memory_space=pltpu.VMEM),
        scratch_shapes=[
            v((NL, 64, 128), F32), v(blocks, F32), v((NL, 128, 128), F32), v(blocks, F32), v((NL, 128, 128), F32),
            v(blocks, F32), v(blocks, F32), v(slices, F32), v(slices, F32), v(slices, F32), v(slices, F32),
            v(slices, F32), v(parts, F32), v(parts, F32), v((NL, 8, 128), F32),
            v((2, NS, 8, 128), F32), v((NHELD, 128, 128), F32), v((NHELD // 2, 128, 256), BF16), v((NHELD // 2, 128, 256), BF16),
            v((NGATHERED, 2, 8, 128), F32), v((7, 2, 8, 128), F32),
            v((NP, 2, 8, 128), F32), v((NP, 2, 8, 128), F32), v((NP, 2, 2, 8, 128), F32),
            v((NP, 2, 8, 128), F32), v((NP, 3, 2, 8, 128), F32), v((NP, 3, 2, 8, 128), F32),
            dma((9,)), dma((NL,)), dma((NL,)), dma((NL,)), dma((NL,)), dma((len(HELD),)), dma((len(GATHERED),)), dma((6,)), dma, dma, dma,
            dma((NP,)), dma((NL,)), dma((NL,)), dma((NL,)), dma((len(HELD),)), dma((len(GATHERED),)), dma((6,)),
            dma((NL,)), dma((NL,)),
        ],
        compiler_params=pltpu.CompilerParams(
            collective_id=0, has_side_effects=True, vmem_limit_bytes=60 * 1024 * 1024
        ),
        name="substitution",
    )(
        lower_pattern.transpose(2, 3, 1, 0).reshape(3, 1, NL), upper_pattern.transpose(2, 3, 1, 0).reshape(3, 1, NL), rhs.reshape(NL, 64, 128),
        lower.reshape(blocks), lower_inv.reshape(NL, 128, 128), upper.reshape(blocks), upper_inv.reshape(NL, 128, 128),
    )
    return got.reshape(NL, 1, 64, 128)


def solution(mesh):
    in_specs = (
        P(None, "prow", None, None),
        P(None, "prow", None, "pcol", None, None),
        P(None, "prow", None, "pcol"),
        P(None, "prow", None, None),
        P(None, "prow", None, "pcol", None, None),
        P(None, "prow", None, "pcol"),
        P(None, "prow", None, None),
    )
    out_specs = P(None, "prow", None, None)
    return jax.shard_map(shards, mesh=mesh, in_specs=in_specs, out_specs=out_specs, check_vma=False)
```

```python
import functools

import jax
import jax.numpy as jnp
from jax import lax
from jax.experimental import pallas as pl
from jax.experimental.pallas import tpu as pltpu
from jax.sharding import PartitionSpec as P

MESH = pl.DeviceIdType.MESH
NL = 6
NP = 16
NS = 8
NT = 4
TR = 16
BF16 = jnp.bfloat16
F32 = jnp.float32


def mm_t(x, w):
    return lax.dot_general(
        x, w, (((1,), (1,)), ((), ())),
        precision=lax.Precision.HIGHEST, preferred_element_type=F32,
    )


def mm(a, b):
    return lax.dot_general(
        a, b, (((1,), (0,)), ((), ())),
        precision=lax.Precision.HIGHEST, preferred_element_type=F32,
    )


HELD = {}
for _row, _col in ((5, 4), (4, 5), (3, 4), (2, 3), (1, 3), (0, 3), (1, 2), (0, 2), (0, 1)):
    HELD[_row, _col] = (sum(n for _, n in HELD.values()), min(NP, 1 << _col))
NHELD = sum(n for _, n in HELD.values())
GROUP = {key: i for i, key in enumerate(HELD)}
GATHERED = {"x4": (0, 16), "z5": (16, 16), "z4": (32, 16), "z3": (48, 8), "z2": (56, 4), "z1": (60, 2)}
STEP = {key: i for i, key in enumerate(GATHERED)}
NGATHERED = 62


def split(x):
    high = x.astype(BF16)
    return high, (x - high.astype(F32)).astype(BF16)


def dot_t(x, w):
    return lax.dot_general(x, w, (((1,), (1,)), ((), ())), preferred_element_type=F32)


def width(level):
    return min(NP, 1 << level)


def kernel(
    lpat, upat, rhs_h, low_h, linv_h, upp_h, uinv_h, out,
    rhs, low, linv, upp, uinv, mf, mb, accf, accb, xf, xb, pf, ca, cb, own,
    e1, m21, held, wh, wl, seen, mine, r4, r5, r45, d3, d5, d4,
    s_in, s_x, s_z, s_ca, s_cb, s_held, s_seen, s_rows, s_out, s_e1, t_e1, s_m21, t_m21,
    t_x0, t_a, t_b, t_ag, t_held, t_seen, t_rows, t_z, t_out,
):
    r = lax.axis_index("prow")
    c = lax.axis_index("pcol")
    par, q = c // NP, lax.rem(c, NP)
    even, odd = par == 0, par == 1
    dy = lax.rem(r // 2 - q // 2 + 9, 8)
    owner = dy < 4
    slot = jnp.where(owner, dy * 2 + lax.rem(r, 2), 0)
    diag = r == q

    def seat(k, row):
        return 8 * (2 * lax.rem(k, 2) + lax.rem(row, 2)) + 4 * (k // 2) + 2 * lax.rem(k, 2)

    def tail_seat(k, row):
        return seat(k, row) + 1

    col_x, col_z = c // 8, lax.rem(c, 8)
    half = col_x // 2
    turned = lax.rem(col_z + 8 - 2 * half, 8)
    seated = lax.rem(col_x, 2) == lax.rem(r, 2)
    team = jnp.logical_and(seated, lax.rem(turned, 4) == 0)
    tail = jnp.logical_and(seated, lax.rem(turned, 4) == 1)
    k_me = jnp.where(jnp.logical_or(team, tail), half + 2 * (turned // 4), 0)

    def same(level):
        return r // width(level) == q // width(level)

    def near(position, j):
        return lax.rem(position // 2 + j // 2 + 7, 8) * 2 + lax.rem(j, 2)

    def at(row, col):
        return {"prow": row, "pcol": col}

    barrier = pltpu.get_barrier_semaphore()

    def tell(row, col):
        @pl.when(jnp.logical_not(jnp.logical_and(row == r, col == c)))
        def _():
            pl.semaphore_signal(barrier, inc=1, device_id=at(row, col), device_id_type=MESH)

    @pl.loop(0, NS)
    def _(j):
        tell(near(q, j), c)

    @pl.loop(0, NT)
    def _(k):
        tell(r, seat(k, r))
        tell(r, tail_seat(k, r))
        tell(q, seat(k, q))

    @pl.when(jnp.logical_and(even, same(2)))
    def _():
        tell(r, NP + q)

    @pl.when(owner)
    def _():
        @pl.loop(0, 2 * NP)
        def _(k):
            tell(q, k)

    @pl.when(jnp.logical_or(team, tail))
    def _():
        @pl.loop(0, 2 * NP)
        def _(k):
            tell(r, k)

    @pl.when(team)
    def _():
        @pl.loop(0, NP)
        def _(k):
            tell(k, seat(k_me, k))

    @pl.when(tail)
    def _():
        @pl.loop(0, 8)
        def _(d):
            row = jnp.bitwise_xor(r, d)
            tell(row, seat(k_me, row))

        @pl.loop(1, 4)
        def _(d):
            row = jnp.bitwise_xor(r, d)
            tell(row, tail_seat(k_me, row))

    loads = [(rhs_h, rhs), (linv_h, linv), (uinv_h, uinv)]
    for m in range(3):
        loads.append((low_h.at[pl.ds(2 * m + 1, 5 - 2 * m), m], low.at[pl.ds(2 * m + 1, 5 - 2 * m), m]))
    for m in range(3):
        loads.append((upp_h.at[pl.ds(0, 2 * m + 1), m], upp.at[pl.ds(0, 2 * m + 1), m]))
    copies = [pltpu.make_async_copy(a, b, s_in.at[i]) for i, (a, b) in enumerate(loads)]
    for copy in copies:
        copy.start()

    accf[...] = jnp.zeros_like(accf)
    accb[...] = jnp.zeros_like(accb)
    for copy in copies[:6]:
        copy.wait()

    top = mm(uinv[5], linv[5])

    def fold(inv, block, bit):
        return mm(inv, block * bit.astype(F32))

    for m in range(3):
        for row in range(2 * m + 1, NL):
            mf[row, m] = fold(top if row == 5 else linv[row], low[row, m], lpat[m, 0, row])

    @pl.when(diag)
    def _():
        for row in range(1, NL):
            @pl.when(par == (0 if row == 2 else (row - 1) % 2))
            def _(row=row):
                accf[row] = mm_t(rhs[row], top if row == 5 else linv[row]).reshape(NS, 8, 128)

        @pl.when(even)
        def _():
            xf[0] = mm_t(rhs[0], linv[0]).reshape(NS, 8, 128)

    one = jnp.where(diag, 1, 0)
    seats = 2 * NT - jnp.where(jnp.logical_or(team, tail), 1, 0)
    expected = 2 * NS - one + jnp.where(owner, NP - 1, 0) + seats
    expected = expected + jnp.where(team, 2 * NP - 1 + NP - 1 + 2 * NP - one + 8, 0)
    expected = expected + jnp.where(tail, 2 * NP - 1 + 3, 0)
    expected = expected + jnp.where(jnp.logical_and(odd, same(2)), 1, 0)
    pl.semaphore_wait(barrier, expected)

    def wait_bytes(ref, sem):
        pltpu.make_async_copy(ref, ref, sem).wait()

    def push(source, target, send_sem, recv_sem, row, col, may_be_me):
        def remote():
            pltpu.make_async_remote_copy(
                source, target, send_sem, recv_sem, device_id=at(row, col), device_id_type=MESH
            ).start()

        if not may_be_me:
            remote()
            return
        me = jnp.logical_and(row == r, col == c)
        pl.when(jnp.logical_not(me))(remote)

        @pl.when(me)
        def _():
            pltpu.make_async_copy(source, target, recv_sem).start()

    @pl.when(jnp.logical_and(diag, even))
    def _():
        @pl.loop(1, NP)
        def _(d):
            push(xf.at[0], xf.at[0], t_x0.at[d], s_x.at[0], jnp.bitwise_xor(r, d), c, False)

    def to_owners(source, target, place, send_sem, recv_sem, parity):
        for j in (6, 7, 0, 1, 4, 5, 2, 3):
            push(source.at[j], target.at[place], send_sem, recv_sem, near(r, j), parity * NP + r, parity is par)

    def to_team(piece, target, send_sem, recv_sem, where):
        for k in range(NT):
            push(piece(pl.ds(2 * k, 2)), target, send_sem, recv_sem, r, where(k, r), True)

    def wait_slices(ref, sem):
        @pl.when(owner)
        def _():
            wait_bytes(ref.at[pl.ds(0, NS - 1)], sem)

        @pl.when(jnp.logical_not(owner))
        def _():
            wait_bytes(ref, sem)

    def give(row, col, source):
        first, n = HELD[row, col]
        i = GROUP[row, col]
        where = seat if row > 2 else tail_seat

        @pl.when(same(col))
        def _():
            @pl.loop(0, NT)
            def _(k):
                push(source, held.at[first + lax.rem(q, n)], t_held.at[i], s_held.at[i], r, where(k, r), True)

    def minus(ref, row, x, w):
        ref[row] = ref[row] - mm_t(x, w).reshape(NS, 8, 128)

    def forward_hold(level):
        m = level // 2
        if level == 0:
            @pl.when(jnp.logical_not(diag))
            def _():
                wait_bytes(xf.at[0], s_x.at[0])
        else:
            wait_slices(xf.at[level], s_x.at[level])
        x = xf[level].reshape(64, 128)
        if level < 3:
            if level != 1:
                @pl.when(same(level + 1))
                def _():
                    row = level + 1
                    pf[level] = accf[row] - mm_t(x, mf[row, m]).reshape(NS, 8, 128)
                    if level == 0:
                        for d in range(4):
                            push(
                                pf.at[0], e1.at[lax.rem(q, 2)], t_e1, s_e1,
                                jnp.bitwise_xor(r, d), r, True,
                            )
                    to_owners(
                        pf.at[level], ca, row * NP + lax.rem(q, width(row)), t_a.at[row], s_ca.at[row], 1 - par
                    )

            row = level + 2
            if row < 4:
                @pl.when(same(row))
                def _():
                    minus(accf, row, x, mf[row, m])
                    if row == 3:
                        to_owners(accf.at[row], cb, row * NP + lax.rem(q, width(row)), t_b.at[row], s_cb.at[row], par)

            for row in range(level + 3, 4):
                @pl.when(same(row))
                def _(row=row):
                    minus(accf, row, x, mf[row, m])

            minus(accf, 4, x, mf[4, m])
            minus(accf, 5, x, mf[5, m])
            if level == 2:
                to_team(lambda k: accf.at[pl.ds(4, 2), k], r45.at[q], t_rows.at[0], s_rows.at[0], seat)
        else:
            minus(accf, 4, x, mf[4, m])
            to_team(lambda k: accf.at[4, k], r4.at[q], t_rows.at[1], s_rows.at[1], seat)
            minus(accf, 5, x, mf[5, m])
            to_team(lambda k: accf.at[5, k], r5.at[q], t_rows.at[2], s_rows.at[2], seat)

        @pl.when(diag)
        def _():
            accb[level] = mm_t(x, uinv[level]).reshape(NS, 8, 128)

    def forward_second():
        wait_bytes(e1, s_e1)
        x = (e1[0] + e1[1]).reshape(64, 128)
        wait_bytes(m21, s_m21)
        pf[1] = accf[2] - mm_t(x, m21[...]).reshape(NS, 8, 128)
        to_owners(pf.at[1], ca, 2 * NP + lax.rem(q, 4), t_a.at[2], s_ca.at[2], par)

    def forward_own(level):
        n = width(level)
        wait_bytes(ca.at[pl.ds(level * NP, n)], s_ca.at[level])
        total = jnp.sum(ca[level * NP:level * NP + n], axis=0)
        if level >= 3:
            wait_bytes(cb.at[pl.ds(level * NP, n)], s_cb.at[level])
            total = total + jnp.sum(cb[level * NP:level * NP + n], axis=0)
        own[level] = total
        xf[level, slot] = total

        @pl.loop(1, NP)
        def _(d):
            row = jnp.bitwise_xor(r, NP - d)
            push(own.at[level], xf.at[level, slot], t_ag.at[level], s_x.at[level], row, c, False)

    def prepare_back():
        for copy in copies[6:]:
            copy.wait()
        for m in range(3):
            for row in range(0, 2 * m + 1):
                mb[row, m] = fold(uinv[row], upp[row, m], upat[m, 0, row])

    @pl.when(even)
    def _():
        forward_hold(0)
        pl.when(same(2))(forward_second)
        give(5, 4, mf.at[5, 2])
        prepare_back()
        pl.when(owner)(functools.partial(forward_own, 2))
        forward_hold(2)
        give(3, 4, mb.at[3, 2])
        give(1, 2, mb.at[1, 1])
        give(0, 2, mb.at[0, 1])

    @pl.when(odd)
    def _():
        @pl.when(same(2))
        def _():
            push(mf.at[2, 0], m21, t_m21, s_m21, r, q, False)

        prepare_back()
        give(4, 5, mb.at[4, 2])
        pl.when(owner)(functools.partial(forward_own, 1))
        forward_hold(1)
        give(2, 3, mb.at[2, 1])
        give(1, 3, mb.at[1, 1])
        pl.when(owner)(functools.partial(forward_own, 3))
        forward_hold(3)
        give(0, 3, mb.at[0, 1])
        give(0, 1, mb.at[0, 0])

    def take(row, col):
        first, n = HELD[row, col]
        wait_bytes(held.at[pl.ds(first, n)], s_held.at[GROUP[row, col]])
        for i in range(first // 2, (first + n) // 2):
            high, low_ = split(jnp.concatenate([held[2 * i], held[2 * i + 1]], axis=1))
            wh[i] = high
            wl[i] = low_

    def apply(row, col, name):
        first, n = HELD[row, col]
        base, _ = GATHERED[name]
        total = jnp.zeros((TR, 128), F32)
        for i in range(n // 2):
            high, low_ = split(jnp.concatenate(
                [seen[base + 2 * i].reshape(TR, 128), seen[base + 2 * i + 1].reshape(TR, 128)], axis=1
            ))
            both = dot_t(jnp.concatenate([high, low_], axis=0), wh[first // 2 + i])
            total = total + both[0:TR] + both[TR:2 * TR] + dot_t(high, wl[first // 2 + i])
        return total

    def gather(name, value):
        base, n = GATHERED[name]
        i = STEP[name]
        where = seat if n == NP else tail_seat
        mine[i] = value.reshape(2, 8, 128)
        place = base + lax.rem(r, n)
        if name != "z3":
            seen[place] = value.reshape(2, 8, 128)

        @pl.loop(0 if name == "z3" else 1, n)
        def _(d):
            row = jnp.bitwise_xor(r, n - 1 - d if name == "z3" else n - d)
            push(mine.at[i], seen.at[place], t_seen.at[i], s_seen.at[i], row, where(k_me, row), False)

    def gathered(name):
        base, n = GATHERED[name]
        wait_bytes(seen.at[pl.ds(base, n if name == "z3" else n - 1)], s_seen.at[STEP[name]])

    def to_holders(level, name):
        @pl.loop(0, NP)
        def _(d):
            row = jnp.bitwise_xor(r, NP - 1 - d)
            push(
                mine.at[STEP[name]], xb.at[level, pl.ds(2 * k_me, 2)], t_z.at[level], s_z.at[level],
                row, (level % 2) * NP + r, True,
            )

    def deliver(level, source, n):
        @pl.loop(0, 2 * NP)
        def _(col):
            push(source, out.at[pl.ds(level, n), pl.ds(2 * k_me, 2)], t_out.at[level], s_out, r, col, True)

    @pl.when(team)
    def _():
        wait_bytes(r45, s_rows.at[0])
        before = jnp.sum(r45[...], axis=0).reshape(2, TR, 128)
        wait_bytes(r4, s_rows.at[1])
        x4 = jnp.sum(r4[...], axis=0).reshape(TR, 128) + before[0]
        gather("x4", x4)
        take(5, 4)
        u4 = mm_t(x4, uinv[4])
        wait_bytes(r5, s_rows.at[2])
        z5 = jnp.sum(r5[...], axis=0).reshape(TR, 128) + before[1]
        gathered("x4")
        z5 = z5 - apply(5, 4, "x4")
        gather("z5", z5)
        to_holders(5, "z5")
        deliver(5, mine.at[pl.ds(STEP["z5"], 1)], 1)
        take(4, 5)
        gathered("z5")
        z4 = u4 - apply(4, 5, "z5")
        gather("z4", z4)
        to_holders(4, "z4")
        deliver(4, mine.at[pl.ds(STEP["z4"], 1)], 1)
        take(3, 4)

    @pl.when(odd)
    def _():
        wait_bytes(xb.at[5], s_z.at[5])
        z = xb[5].reshape(64, 128)
        minus(accb, 3, z, mb[3, 2])
        to_team(lambda k: accb.at[3, k], d3.at[q], t_rows.at[3], s_rows.at[3], seat)
        for row in range(3):
            minus(accb, row, z, mb[row, 2])
        to_team(lambda k: accb.at[pl.ds(0, 3), k], d5.at[q], t_rows.at[4], s_rows.at[4], tail_seat)

    @pl.when(team)
    def _():
        wait_bytes(d3, s_rows.at[3])
        z3 = jnp.sum(d3[...], axis=0).reshape(TR, 128)
        gathered("z4")
        z3 = z3 - apply(3, 4, "z4")
        gather("z3", z3)
        deliver(3, mine.at[pl.ds(STEP["z3"], 1)], 1)

    @pl.when(even)
    def _():
        wait_bytes(xb.at[4], s_z.at[4])
        z = xb[4].reshape(64, 128)
        minus(accb, 2, z, mb[2, 2])
        to_team(lambda k: accb.at[2, k], d4.at[q, 2], t_rows.at[6], s_rows.at[6], tail_seat)
        for row in range(2):
            minus(accb, row, z, mb[row, 2])
        to_team(lambda k: accb.at[pl.ds(0, 2), k], d4.at[q, pl.ds(0, 2)], t_rows.at[5], s_rows.at[5], tail_seat)

    @pl.when(tail)
    def _():
        take(2, 3)
        take(1, 3)
        take(1, 2)
        wait_bytes(d5, s_rows.at[4])
        late = jnp.sum(d5[...], axis=0).reshape(3, TR, 128)
        gathered("z3")
        late2 = late[2] - apply(2, 3, "z3")
        late1 = late[1] - apply(1, 3, "z3")
        wait_bytes(r4, s_rows.at[6])
        gather("z2", late2 + jnp.sum(d4[:, 2], axis=0).reshape(TR, 128))
        deliver(2, mine.at[pl.ds(STEP["z2"], 1)], 1)
        wait_bytes(r45, s_rows.at[5])
        last = jnp.sum(d4[:, 0:2], axis=0).reshape(2, TR, 128)
        take(0, 3)
        take(0, 2)
        take(0, 1)
        late0 = late[0] + last[0] - apply(0, 3, "z3")
        gathered("z2")
        gather("z1", late1 + last[1] - apply(1, 2, "z2"))
        late0 = late0 - apply(0, 2, "z2")
        deliver(1, mine.at[pl.ds(STEP["z1"], 1)], 1)
        gathered("z1")
        mine[6] = (late0 - apply(0, 1, "z1")).reshape(2, 8, 128)
        for dx in (2, 1, 3, 0):
            for dz in (4, 3, 5, 2, 6, 1, 7, 0):
                col = 8 * lax.rem(col_x + dx, 4) + lax.rem(col_z + dz, 8)
                piece = out.at[pl.ds(0, 1), pl.ds(2 * k_me, 2)]
                if dx == dz == 0:
                    pltpu.make_async_copy(mine.at[pl.ds(6, 1)], piece, s_out).start()
                else:
                    push(mine.at[pl.ds(6, 1)], piece, t_out.at[0], s_out, r, col, False)

    @pl.when(jnp.logical_and(diag, even))
    def _():
        @pl.loop(1, NP)
        def _(d):
            wait_bytes(xf.at[0], t_x0.at[d])

    def slices(n):
        return ca.at[pl.ds(0, n)]

    def sent_slices(sem, n):
        @pl.when(diag)
        def _():
            wait_bytes(slices(n - 1), sem)

        @pl.when(jnp.logical_not(diag))
        def _():
            wait_bytes(slices(n), sem)

    @pl.when(jnp.logical_and(even, same(1)))
    def _():
        wait_bytes(slices(NS), t_a.at[1])

        @pl.when(diag)
        def _():
            wait_bytes(xf.at[pl.ds(0, 3)], t_e1)

        @pl.when(jnp.logical_not(diag))
        def _():
            wait_bytes(xf.at[pl.ds(0, 4)], t_e1)

    @pl.when(jnp.logical_and(even, same(2)))
    def _():
        sent_slices(t_a.at[2], NS)

    @pl.when(jnp.logical_and(even, same(3)))
    def _():
        wait_bytes(slices(NS), t_a.at[3])

    @pl.when(jnp.logical_and(odd, same(2)))
    def _():
        wait_bytes(m21, t_m21)

    @pl.when(jnp.logical_and(odd, same(3)))
    def _():
        sent_slices(t_b.at[3], NS)

    for row in range(1, 4):
        @pl.when(jnp.logical_and(par == row % 2, owner))
        def _(row=row):
            wait_bytes(slices(NP - 1), t_ag.at[row])

    def sent_rows(i, n):
        kept = tail if i > 3 else team

        @pl.when(kept)
        def _():
            wait_bytes(slices(2 * (NT - 1) * n), t_rows.at[i])

        @pl.when(jnp.logical_not(kept))
        def _():
            wait_bytes(slices(2 * NT * n), t_rows.at[i])

    def sent_blocks(row, col):
        @pl.when(same(col))
        def _():
            i = GROUP[row, col]
            kept = team if row > 2 else tail

            @pl.when(kept)
            def _():
                wait_bytes(held.at[pl.ds(0, NT - 1)], t_held.at[i])

            @pl.when(jnp.logical_not(kept))
            def _():
                wait_bytes(held.at[pl.ds(0, NT)], t_held.at[i])

    @pl.when(even)
    def _():
        sent_rows(0, 2)
        sent_rows(5, 2)
        sent_rows(6, 1)
        for key in ((5, 4), (3, 4), (1, 2), (0, 2)):
            sent_blocks(*key)

    @pl.when(odd)
    def _():
        sent_rows(1, 1)
        sent_rows(2, 1)
        sent_rows(3, 1)
        sent_rows(4, 3)
        for key in ((4, 5), (2, 3), (1, 3), (0, 3), (0, 1)):
            sent_blocks(*key)

    @pl.when(team)
    def _():
        for name in ("x4", "z5", "z4"):
            wait_bytes(slices(2 * (NP - 1)), t_seen.at[STEP[name]])
        wait_bytes(slices(2 * 8), t_seen.at[STEP["z3"]])
        for level in (5, 4):
            own_seat = jnp.logical_and(diag, par == level % 2)

            @pl.when(own_seat)
            def _(level=level):
                wait_bytes(slices(2 * (NP - 1)), t_z.at[level])

            @pl.when(jnp.logical_not(own_seat))
            def _(level=level):
                wait_bytes(slices(2 * NP), t_z.at[level])
        for level in (5, 4, 3):
            wait_bytes(slices(2 * (2 * NP - 1)), t_out.at[level])

    @pl.when(tail)
    def _():
        wait_bytes(slices(2 * 3), t_seen.at[STEP["z2"]])
        wait_bytes(slices(2 * 1), t_seen.at[STEP["z1"]])
        for level in (2, 1, 0):
            wait_bytes(slices(2 * (2 * NP - 1)), t_out.at[level])

    wait_bytes(out, s_out)


def shards(rhs, lower, lower_pattern, lower_inv, upper, upper_pattern, upper_inv):
    v = pltpu.VMEM
    dma = pltpu.SemaphoreType.DMA
    slices = (NL, NS, 8, 128)
    parts = (NL * NP, 8, 128)
    blocks = (NL, 3, 128, 128)
    got = pl.pallas_call(
        kernel,
        out_shape=jax.ShapeDtypeStruct(slices, F32),
        in_specs=[pl.BlockSpec(memory_space=pltpu.SMEM)] * 2 + [pl.BlockSpec(memory_space=pl.ANY)] * 5,
        out_specs=pl.BlockSpec(memory_space=pltpu.VMEM),
        scratch_shapes=[
            v((NL, 64, 128), F32), v(blocks, F32), v((NL, 128, 128), F32), v(blocks, F32), v((NL, 128, 128), F32),
            v(blocks, F32), v(blocks, F32), v(slices, F32), v(slices, F32), v(slices, F32), v(slices, F32),
            v(slices, F32), v(parts, F32), v(parts, F32), v((NL, 8, 128), F32),
            v((2, NS, 8, 128), F32), v((128, 128), F32), v((NHELD, 128, 128), F32), v((NHELD // 2, 128, 256), BF16), v((NHELD // 2, 128, 256), BF16),
            v((NGATHERED, 2, 8, 128), F32), v((7, 2, 8, 128), F32),
            v((NP, 2, 8, 128), F32), v((NP, 2, 8, 128), F32), v((NP, 2, 2, 8, 128), F32),
            v((NP, 2, 8, 128), F32), v((NP, 3, 2, 8, 128), F32), v((NP, 3, 2, 8, 128), F32),
            dma((9,)), dma((NL,)), dma((NL,)), dma((NL,)), dma((NL,)), dma((len(HELD),)), dma((len(GATHERED),)), dma((7,)), dma, dma, dma, dma, dma,
            dma((NP,)), dma((NL,)), dma((NL,)), dma((NL,)), dma((len(HELD),)), dma((len(GATHERED),)), dma((7,)),
            dma((NL,)), dma((NL,)),
        ],
        compiler_params=pltpu.CompilerParams(
            collective_id=0, has_side_effects=True, vmem_limit_bytes=60 * 1024 * 1024
        ),
        name="substitution",
    )(
        lower_pattern.transpose(2, 3, 1, 0).reshape(3, 1, NL), upper_pattern.transpose(2, 3, 1, 0).reshape(3, 1, NL), rhs.reshape(NL, 64, 128),
        lower.reshape(blocks), lower_inv.reshape(NL, 128, 128), upper.reshape(blocks), upper_inv.reshape(NL, 128, 128),
    )
    return got.reshape(NL, 1, 64, 128)


def solution(mesh):
    in_specs = (
        P(None, "prow", None, None),
        P(None, "prow", None, "pcol", None, None),
        P(None, "prow", None, "pcol"),
        P(None, "prow", None, None),
        P(None, "prow", None, "pcol", None, None),
        P(None, "prow", None, "pcol"),
        P(None, "prow", None, None),
    )
    out_specs = P(None, "prow", None, None)
    return jax.shard_map(shards, mesh=mesh, in_specs=in_specs, out_specs=out_specs, check_vma=False)
```

```python
import functools

import jax
import jax.numpy as jnp
from jax import lax
from jax.experimental import pallas as pl
from jax.experimental.pallas import tpu as pltpu
from jax.sharding import PartitionSpec as P

MESH = pl.DeviceIdType.MESH
NL = 6
NP = 16
NS = 8
NT = 4
TR = 16
BF16 = jnp.bfloat16
F32 = jnp.float32


def mm_t(x, w):
    return lax.dot_general(
        x, w, (((1,), (1,)), ((), ())),
        precision=lax.Precision.HIGHEST, preferred_element_type=F32,
    )


def mm(a, b):
    return lax.dot_general(
        a, b, (((1,), (0,)), ((), ())),
        precision=lax.Precision.HIGHEST, preferred_element_type=F32,
    )


HELD = {}
for _row, _col in ((5, 4), (4, 5), (3, 4), (2, 3), (1, 3), (0, 3), (1, 2), (0, 2), (0, 1)):
    HELD[_row, _col] = (sum(n for _, n in HELD.values()), min(NP, 1 << _col))
NHELD = sum(n for _, n in HELD.values())
GROUP = {key: i for i, key in enumerate(HELD)}
GATHERED = {"x4": (0, 16), "z5": (16, 16), "z4": (32, 16), "z3": (48, 8), "z2": (56, 4), "z1": (60, 2)}
STEP = {key: i for i, key in enumerate(GATHERED)}
NGATHERED = 62


def split(x):
    high = x.astype(BF16)
    return high, (x - high.astype(F32)).astype(BF16)


def dot_t(x, w):
    return lax.dot_general(x, w, (((1,), (1,)), ((), ())), preferred_element_type=F32)


def width(level):
    return min(NP, 1 << level)


def kernel(
    lpat, upat, rhs_h, low_h, linv_h, upp_h, uinv_h, out,
    rhs, low, linv, upp, uinv, mf, mb, accf, accb, xf, xb, pf, ca, cb, own,
    e1, m21, held, wh, wl, seen, mine, r4, r5, r45, d3, d5, d4,
    s_in, s_x, s_z, s_ca, s_cb, s_held, s_seen, s_rows, s_out, s_e1, t_e1, s_m21, t_m21,
    t_x0, t_a, t_b, t_ag, t_held, t_seen, t_rows, t_z, t_out,
):
    r = lax.axis_index("prow")
    c = lax.axis_index("pcol")
    par, q = c // NP, lax.rem(c, NP)
    even, odd = par == 0, par == 1
    dy = lax.rem(r // 2 - q // 2 + 9, 8)
    owner = dy < 4
    slot = jnp.where(owner, dy * 2 + lax.rem(r, 2), 0)
    diag = r == q

    def seat(k, row):
        return 8 * (2 * lax.rem(k, 2) + lax.rem(row, 2)) + 4 * (k // 2) + 2 * lax.rem(k, 2)

    def tail_seat(k, row):
        return seat(k, row) + 1

    col_x, col_z = c // 8, lax.rem(c, 8)
    half = col_x // 2
    turned = lax.rem(col_z + 8 - 2 * half, 8)
    team = jnp.logical_and(lax.rem(col_x, 2) == lax.rem(r, 2), lax.rem(turned, 4) == 0)
    k_tail = half + 2 * (turned // 4)
    tail = c == tail_seat(k_tail, r)
    k_me = jnp.where(tail, k_tail, jnp.where(team, half + 2 * (turned // 4), 0))

    def same(level):
        return r // width(level) == q // width(level)

    def near(position, j):
        return lax.rem(position // 2 + j // 2 + 7, 8) * 2 + lax.rem(j, 2)

    def at(row, col):
        return {"prow": row, "pcol": col}

    barrier = pltpu.get_barrier_semaphore()

    def tell(row, col):
        @pl.when(jnp.logical_not(jnp.logical_and(row == r, col == c)))
        def _():
            pl.semaphore_signal(barrier, inc=1, device_id=at(row, col), device_id_type=MESH)

    @pl.loop(0, NT)
    def _(k):
        tell(q, seat(k, q))

    @pl.when(owner)
    def _():
        @pl.loop(0, 2 * NP)
        def _(k):
            tell(q, k)

    @pl.loop(0, NT)
    def _(k):
        tell(r, seat(k, r))
        tell(r, tail_seat(k, r))

    @pl.loop(0, NS)
    def _(j):
        tell(near(q, j), c)

    @pl.when(jnp.logical_and(even, same(2)))
    def _():
        tell(r, NP + q)

    @pl.when(jnp.logical_or(team, tail))
    def _():
        @pl.loop(0, 2 * NP)
        def _(k):
            tell(r, k)

    @pl.when(team)
    def _():
        @pl.loop(0, NP)
        def _(k):
            tell(k, seat(k_me, k))

    @pl.when(tail)
    def _():
        @pl.loop(0, 8)
        def _(d):
            row = jnp.bitwise_xor(r, d)
            tell(row, seat(k_me, row))

        @pl.loop(1, 4)
        def _(d):
            row = jnp.bitwise_xor(r, d)
            tell(row, tail_seat(k_me, row))

    loads = [(rhs_h, rhs), (linv_h, linv), (uinv_h, uinv)]
    for m in range(3):
        loads.append((low_h.at[pl.ds(2 * m + 1, 5 - 2 * m), m], low.at[pl.ds(2 * m + 1, 5 - 2 * m), m]))
    for m in range(3):
        loads.append((upp_h.at[pl.ds(0, 2 * m + 1), m], upp.at[pl.ds(0, 2 * m + 1), m]))
    copies = [pltpu.make_async_copy(a, b, s_in.at[i]) for i, (a, b) in enumerate(loads)]
    for copy in copies:
        copy.start()

    accf[...] = jnp.zeros_like(accf)
    accb[...] = jnp.zeros_like(accb)
    def fold(inv, block, bit):
        return mm(inv, block * bit.astype(F32))

    for i in (0, 1, 3):
        copies[i].wait()
    for row in (1, 2):
        mf[row, 0] = fold(linv[row], low[row, 0], lpat[0, 0, row])

    @pl.when(jnp.logical_and(diag, even))
    def _():
        for row in (1, 2):
            accf[row] = mm_t(rhs[row], linv[row]).reshape(NS, 8, 128)
        xf[0] = mm_t(rhs[0], linv[0]).reshape(NS, 8, 128)

    def prepare_forward():
        top = mm(uinv[5], linv[5])
        for m in range(2):
            for row in range(3, NL):
                mf[row, m] = fold(top if row == 5 else linv[row], low[row, m], lpat[m, 0, row])

        @pl.when(diag)
        def _():
            for row in range(3, NL):
                @pl.when(par == (row - 1) % 2)
                def _(row=row):
                    accf[row] = mm_t(rhs[row], top if row == 5 else linv[row]).reshape(NS, 8, 128)

    one = jnp.where(diag, 1, 0)
    seats = 2 * NT - jnp.where(jnp.logical_or(team, tail), 1, 0)
    expected = 2 * NS - one + jnp.where(owner, NP - 1, 0) + seats
    expected = expected + jnp.where(team, 2 * NP - 1 + NP - 1 + 2 * NP - one + 8, 0)
    expected = expected + jnp.where(tail, 2 * NP - 1 + 3, 0)
    expected = expected + jnp.where(jnp.logical_and(odd, same(2)), 1, 0)
    pl.semaphore_wait(barrier, expected)

    def wait_bytes(ref, sem):
        pltpu.make_async_copy(ref, ref, sem).wait()

    def push(source, target, send_sem, recv_sem, row, col, may_be_me):
        def remote():
            pltpu.make_async_remote_copy(
                source, target, send_sem, recv_sem, device_id=at(row, col), device_id_type=MESH
            ).start()

        if not may_be_me:
            remote()
            return
        me = jnp.logical_and(row == r, col == c)
        pl.when(jnp.logical_not(me))(remote)

        @pl.when(me)
        def _():
            pltpu.make_async_copy(source, target, recv_sem).start()

    @pl.when(jnp.logical_and(diag, even))
    def _():
        @pl.loop(1, NP)
        def _(d):
            push(xf.at[0], xf.at[0], t_x0.at[d], s_x.at[0], jnp.bitwise_xor(r, d), c, False)

    def to_owners(source, target, place, send_sem, recv_sem, parity):
        for j in (6, 7, 0, 1, 4, 5, 2, 3):
            push(source.at[j], target.at[place], send_sem, recv_sem, near(r, j), parity * NP + r, parity is par)

    def to_team(piece, target, send_sem, recv_sem, where):
        for k in range(NT):
            push(piece(pl.ds(2 * k, 2)), target, send_sem, recv_sem, r, where(k, r), True)

    def wait_slices(ref, sem):
        @pl.when(owner)
        def _():
            wait_bytes(ref.at[pl.ds(0, NS - 1)], sem)

        @pl.when(jnp.logical_not(owner))
        def _():
            wait_bytes(ref, sem)

    def give(row, col, source):
        first, n = HELD[row, col]
        i = GROUP[row, col]
        where = seat if row > 2 else tail_seat

        @pl.when(same(col))
        def _():
            @pl.loop(0, NT)
            def _(k):
                push(source, held.at[first + lax.rem(q, n)], t_held.at[i], s_held.at[i], r, where(k, r), True)

    def minus(ref, row, x, w):
        ref[row] = ref[row] - mm_t(x, w).reshape(NS, 8, 128)

    def forward_hold(level):
        m = level // 2
        if level == 0:
            @pl.when(jnp.logical_not(diag))
            def _():
                wait_bytes(xf.at[0], s_x.at[0])
        else:
            wait_slices(xf.at[level], s_x.at[level])
        x = xf[level].reshape(64, 128)
        if level < 3:
            if level != 1:
                @pl.when(same(level + 1))
                def _():
                    row = level + 1
                    pf[level] = accf[row] - mm_t(x, mf[row, m]).reshape(NS, 8, 128)
                    if level == 0:
                        for d in range(4):
                            push(
                                pf.at[0], e1.at[lax.rem(q, 2)], t_e1, s_e1,
                                jnp.bitwise_xor(r, d), r, True,
                            )
                    to_owners(
                        pf.at[level], ca, row * NP + lax.rem(q, width(row)), t_a.at[row], s_ca.at[row], 1 - par
                    )

            if level == 0:
                prepare_forward()
            row = level + 2
            if row < 4:
                @pl.when(same(row))
                def _():
                    minus(accf, row, x, mf[row, m])
                    if row == 3:
                        to_owners(accf.at[row], cb, row * NP + lax.rem(q, width(row)), t_b.at[row], s_cb.at[row], par)

            for row in range(level + 3, 4):
                @pl.when(same(row))
                def _(row=row):
                    minus(accf, row, x, mf[row, m])

            minus(accf, 4, x, mf[4, m])
            minus(accf, 5, x, mf[5, m])
            if level == 2:
                to_team(lambda k: accf.at[pl.ds(4, 2), k], r45.at[q], t_rows.at[0], s_rows.at[0], seat)
        else:
            minus(accf, 4, x, mf[4, m])
            to_team(lambda k: accf.at[4, k], r4.at[q], t_rows.at[1], s_rows.at[1], seat)
            minus(accf, 5, x, mf[5, m])
            to_team(lambda k: accf.at[5, k], r5.at[q], t_rows.at[2], s_rows.at[2], seat)

        @pl.when(diag)
        def _():
            accb[level] = mm_t(x, uinv[level]).reshape(NS, 8, 128)

    def forward_second():
        wait_bytes(e1, s_e1)
        x = (e1[0] + e1[1]).reshape(64, 128)
        wait_bytes(m21, s_m21)
        pf[1] = accf[2] - mm_t(x, m21[...]).reshape(NS, 8, 128)
        to_owners(pf.at[1], ca, 2 * NP + lax.rem(q, 4), t_a.at[2], s_ca.at[2], par)

    def forward_own(level):
        n = width(level)
        wait_bytes(ca.at[pl.ds(level * NP, n)], s_ca.at[level])
        total = jnp.sum(ca[level * NP:level * NP + n], axis=0)
        if level >= 3:
            wait_bytes(cb.at[pl.ds(level * NP, n)], s_cb.at[level])
            total = total + jnp.sum(cb[level * NP:level * NP + n], axis=0)
        own[level] = total
        xf[level, slot] = total

        @pl.loop(1, NP)
        def _(d):
            row = jnp.bitwise_xor(r, NP - d)
            push(own.at[level], xf.at[level, slot], t_ag.at[level], s_x.at[level], row, c, False)

    def prepare_back():
        for m in range(3):
            for row in range(0, min(4, 2 * m + 1)):
                mb[row, m] = fold(uinv[row], upp[row, m], upat[m, 0, row])

    def first_wide():
        mf[5, 2] = fold(mm(uinv[5], linv[5]), low[5, 2], lpat[2, 0, 5])
        give(5, 4, mf.at[5, 2])

    for i in (2, 4, 5, 6, 7, 8):
        copies[i].wait()

    @pl.when(even)
    def _():
        pl.when(jnp.logical_not(same(2)))(first_wide)
        forward_hold(0)

        @pl.when(same(2))
        def _():
            forward_second()
            first_wide()

        prepare_back()
        pl.when(owner)(functools.partial(forward_own, 2))
        forward_hold(2)
        give(3, 4, mb.at[3, 2])
        give(1, 2, mb.at[1, 1])
        give(0, 2, mb.at[0, 1])

    @pl.when(odd)
    def _():
        @pl.when(same(2))
        def _():
            push(mf.at[2, 0], m21, t_m21, s_m21, r, q, False)

        mb[4, 2] = fold(uinv[4], upp[4, 2], upat[2, 0, 4])
        give(4, 5, mb.at[4, 2])
        prepare_forward()
        prepare_back()
        pl.when(owner)(functools.partial(forward_own, 1))
        forward_hold(1)
        give(2, 3, mb.at[2, 1])
        give(1, 3, mb.at[1, 1])
        pl.when(owner)(functools.partial(forward_own, 3))
        forward_hold(3)
        give(0, 3, mb.at[0, 1])
        give(0, 1, mb.at[0, 0])

    def take(row, col):
        first, n = HELD[row, col]
        wait_bytes(held.at[pl.ds(first, n)], s_held.at[GROUP[row, col]])
        for i in range(first // 2, (first + n) // 2):
            high, low_ = split(jnp.concatenate([held[2 * i], held[2 * i + 1]], axis=1))
            wh[i] = high
            wl[i] = low_

    def apply(row, col, name):
        first, n = HELD[row, col]
        base, _ = GATHERED[name]
        total = jnp.zeros((TR, 128), F32)
        for i in range(n // 2):
            high, low_ = split(jnp.concatenate(
                [seen[base + 2 * i].reshape(TR, 128), seen[base + 2 * i + 1].reshape(TR, 128)], axis=1
            ))
            both = dot_t(jnp.concatenate([high, low_], axis=0), wh[first // 2 + i])
            total = total + both[0:TR] + both[TR:2 * TR] + dot_t(high, wl[first // 2 + i])
        return total

    def gather(name, value):
        base, n = GATHERED[name]
        i = STEP[name]
        where = seat if n == NP else tail_seat
        mine[i] = value.reshape(2, 8, 128)
        place = base + lax.rem(r, n)
        if name != "z3":
            seen[place] = value.reshape(2, 8, 128)

        @pl.loop(0 if name == "z3" else 1, n)
        def _(d):
            row = jnp.bitwise_xor(r, n - 1 - d if name == "z3" else n - d)
            push(mine.at[i], seen.at[place], t_seen.at[i], s_seen.at[i], row, where(k_me, row), False)

    def gathered(name):
        base, n = GATHERED[name]
        wait_bytes(seen.at[pl.ds(base, n if name == "z3" else n - 1)], s_seen.at[STEP[name]])

    def to_holders(level, name):
        @pl.loop(0, NP)
        def _(d):
            row = jnp.bitwise_xor(r, NP - 1 - d)
            push(
                mine.at[STEP[name]], xb.at[level, pl.ds(2 * k_me, 2)], t_z.at[level], s_z.at[level],
                row, (level % 2) * NP + r, True,
            )

    def deliver(level, source, n):
        @pl.loop(0, 2 * NP)
        def _(col):
            push(source, out.at[pl.ds(level, n), pl.ds(2 * k_me, 2)], t_out.at[level], s_out, r, col, True)

    def deliver_far_first(level, source):
        target = out.at[pl.ds(level, 1), pl.ds(2 * k_me, 2)]
        for dx in (2, 1, 3, 0):
            for dz in (4, 3, 5, 2, 6, 1, 7, 0):
                if dx == dz == 0:
                    pltpu.make_async_copy(source, target, s_out).start()
                else:
                    col = 8 * lax.rem(col_x + dx, 4) + lax.rem(col_z + dz, 8)
                    push(source, target, t_out.at[level], s_out, r, col, False)

    @pl.when(team)
    def _():
        wait_bytes(r45, s_rows.at[0])
        before = jnp.sum(r45[...], axis=0).reshape(2, TR, 128)
        wait_bytes(r4, s_rows.at[1])
        x4 = jnp.sum(r4[...], axis=0).reshape(TR, 128) + before[0]
        gather("x4", x4)
        take(5, 4)
        u4 = mm_t(x4, uinv[4])
        wait_bytes(r5, s_rows.at[2])
        z5 = jnp.sum(r5[...], axis=0).reshape(TR, 128) + before[1]
        gathered("x4")
        z5 = z5 - apply(5, 4, "x4")
        gather("z5", z5)
        to_holders(5, "z5")
        deliver(5, mine.at[pl.ds(STEP["z5"], 1)], 1)
        take(4, 5)
        gathered("z5")
        z4 = u4 - apply(4, 5, "z5")
        gather("z4", z4)
        to_holders(4, "z4")
        deliver(4, mine.at[pl.ds(STEP["z4"], 1)], 1)
        take(3, 4)

    @pl.when(odd)
    def _():
        wait_bytes(xb.at[5], s_z.at[5])
        z = xb[5].reshape(64, 128)
        minus(accb, 3, z, mb[3, 2])
        to_team(lambda k: accb.at[3, k], d3.at[q], t_rows.at[3], s_rows.at[3], seat)
        for row in range(3):
            minus(accb, row, z, mb[row, 2])
        to_team(lambda k: accb.at[pl.ds(0, 3), k], d5.at[q], t_rows.at[4], s_rows.at[4], tail_seat)

    @pl.when(team)
    def _():
        wait_bytes(d3, s_rows.at[3])
        z3 = jnp.sum(d3[...], axis=0).reshape(TR, 128)
        gathered("z4")
        z3 = z3 - apply(3, 4, "z4")
        gather("z3", z3)
        deliver(3, mine.at[pl.ds(STEP["z3"], 1)], 1)

    @pl.when(even)
    def _():
        wait_bytes(xb.at[4], s_z.at[4])
        z = xb[4].reshape(64, 128)
        minus(accb, 2, z, mb[2, 2])
        to_team(lambda k: accb.at[2, k], d4.at[q, 2], t_rows.at[6], s_rows.at[6], tail_seat)
        for row in range(2):
            minus(accb, row, z, mb[row, 2])
        to_team(lambda k: accb.at[pl.ds(0, 2), k], d4.at[q, pl.ds(0, 2)], t_rows.at[5], s_rows.at[5], tail_seat)

    @pl.when(tail)
    def _():
        take(2, 3)
        take(1, 3)
        take(1, 2)
        wait_bytes(d5, s_rows.at[4])
        late = jnp.sum(d5[...], axis=0).reshape(3, TR, 128)
        gathered("z3")
        late2 = late[2] - apply(2, 3, "z3")
        late1 = late[1] - apply(1, 3, "z3")
        take(0, 3)
        take(0, 2)
        take(0, 1)
        late0 = late[0] - apply(0, 3, "z3")
        wait_bytes(r4, s_rows.at[6])
        gather("z2", late2 + jnp.sum(d4[:, 2], axis=0).reshape(TR, 128))
        deliver(2, mine.at[pl.ds(STEP["z2"], 1)], 1)
        wait_bytes(r45, s_rows.at[5])
        last = jnp.sum(d4[:, 0:2], axis=0).reshape(2, TR, 128)
        late0 = late0 + last[0]
        gathered("z2")
        gather("z1", late1 + last[1] - apply(1, 2, "z2"))
        late0 = late0 - apply(0, 2, "z2")
        deliver_far_first(1, mine.at[pl.ds(STEP["z1"], 1)])
        gathered("z1")
        mine[6] = (late0 - apply(0, 1, "z1")).reshape(2, 8, 128)
        deliver_far_first(0, mine.at[pl.ds(6, 1)])

    @pl.when(jnp.logical_and(diag, even))
    def _():
        @pl.loop(1, NP)
        def _(d):
            wait_bytes(xf.at[0], t_x0.at[d])

    def slices(n):
        return ca.at[pl.ds(0, n)]

    def sent_slices(sem, n):
        @pl.when(diag)
        def _():
            wait_bytes(slices(n - 1), sem)

        @pl.when(jnp.logical_not(diag))
        def _():
            wait_bytes(slices(n), sem)

    @pl.when(jnp.logical_and(even, same(1)))
    def _():
        wait_bytes(slices(NS), t_a.at[1])

        @pl.when(diag)
        def _():
            wait_bytes(xf.at[pl.ds(0, 3)], t_e1)

        @pl.when(jnp.logical_not(diag))
        def _():
            wait_bytes(xf.at[pl.ds(0, 4)], t_e1)

    @pl.when(jnp.logical_and(even, same(2)))
    def _():
        sent_slices(t_a.at[2], NS)

    @pl.when(jnp.logical_and(even, same(3)))
    def _():
        wait_bytes(slices(NS), t_a.at[3])

    @pl.when(jnp.logical_and(odd, same(2)))
    def _():
        wait_bytes(m21, t_m21)

    @pl.when(jnp.logical_and(odd, same(3)))
    def _():
        sent_slices(t_b.at[3], NS)

    for row in range(1, 4):
        @pl.when(jnp.logical_and(par == row % 2, owner))
        def _(row=row):
            wait_bytes(slices(NP - 1), t_ag.at[row])

    def sent_rows(i, n):
        kept = tail if i > 3 else team

        @pl.when(kept)
        def _():
            wait_bytes(slices(2 * (NT - 1) * n), t_rows.at[i])

        @pl.when(jnp.logical_not(kept))
        def _():
            wait_bytes(slices(2 * NT * n), t_rows.at[i])

    def sent_blocks(row, col):
        @pl.when(same(col))
        def _():
            i = GROUP[row, col]
            kept = team if row > 2 else tail

            @pl.when(kept)
            def _():
                wait_bytes(held.at[pl.ds(0, NT - 1)], t_held.at[i])

            @pl.when(jnp.logical_not(kept))
            def _():
                wait_bytes(held.at[pl.ds(0, NT)], t_held.at[i])

    @pl.when(even)
    def _():
        sent_rows(0, 2)
        sent_rows(5, 2)
        sent_rows(6, 1)
        for key in ((5, 4), (3, 4), (1, 2), (0, 2)):
            sent_blocks(*key)

    @pl.when(odd)
    def _():
        sent_rows(1, 1)
        sent_rows(2, 1)
        sent_rows(3, 1)
        sent_rows(4, 3)
        for key in ((4, 5), (2, 3), (1, 3), (0, 3), (0, 1)):
            sent_blocks(*key)

    @pl.when(team)
    def _():
        for name in ("x4", "z5", "z4"):
            wait_bytes(slices(2 * (NP - 1)), t_seen.at[STEP[name]])
        wait_bytes(slices(2 * 8), t_seen.at[STEP["z3"]])
        for level in (5, 4):
            own_seat = jnp.logical_and(diag, par == level % 2)

            @pl.when(own_seat)
            def _(level=level):
                wait_bytes(slices(2 * (NP - 1)), t_z.at[level])

            @pl.when(jnp.logical_not(own_seat))
            def _(level=level):
                wait_bytes(slices(2 * NP), t_z.at[level])
        for level in (5, 4, 3):
            wait_bytes(slices(2 * (2 * NP - 1)), t_out.at[level])

    @pl.when(tail)
    def _():
        wait_bytes(slices(2 * 3), t_seen.at[STEP["z2"]])
        wait_bytes(slices(2 * 1), t_seen.at[STEP["z1"]])
        for level in (2, 1, 0):
            wait_bytes(slices(2 * (2 * NP - 1)), t_out.at[level])

    wait_bytes(out, s_out)


def shards(rhs, lower, lower_pattern, lower_inv, upper, upper_pattern, upper_inv):
    v = pltpu.VMEM
    dma = pltpu.SemaphoreType.DMA
    slices = (NL, NS, 8, 128)
    parts = (NL * NP, 8, 128)
    blocks = (NL, 3, 128, 128)
    got = pl.pallas_call(
        kernel,
        out_shape=jax.ShapeDtypeStruct(slices, F32),
        in_specs=[pl.BlockSpec(memory_space=pltpu.SMEM)] * 2 + [pl.BlockSpec(memory_space=pl.ANY)] * 5,
        out_specs=pl.BlockSpec(memory_space=pltpu.VMEM),
        scratch_shapes=[
            v((NL, 64, 128), F32), v(blocks, F32), v((NL, 128, 128), F32), v(blocks, F32), v((NL, 128, 128), F32),
            v(blocks, F32), v(blocks, F32), v(slices, F32), v(slices, F32), v(slices, F32), v(slices, F32),
            v(slices, F32), v(parts, F32), v(parts, F32), v((NL, 8, 128), F32),
            v((2, NS, 8, 128), F32), v((128, 128), F32), v((NHELD, 128, 128), F32), v((NHELD // 2, 128, 256), BF16), v((NHELD // 2, 128, 256), BF16),
            v((NGATHERED, 2, 8, 128), F32), v((7, 2, 8, 128), F32),
            v((NP, 2, 8, 128), F32), v((NP, 2, 8, 128), F32), v((NP, 2, 2, 8, 128), F32),
            v((NP, 2, 8, 128), F32), v((NP, 3, 2, 8, 128), F32), v((NP, 3, 2, 8, 128), F32),
            dma((9,)), dma((NL,)), dma((NL,)), dma((NL,)), dma((NL,)), dma((len(HELD),)), dma((len(GATHERED),)), dma((7,)), dma, dma, dma, dma, dma,
            dma((NP,)), dma((NL,)), dma((NL,)), dma((NL,)), dma((len(HELD),)), dma((len(GATHERED),)), dma((7,)),
            dma((NL,)), dma((NL,)),
        ],
        compiler_params=pltpu.CompilerParams(
            collective_id=0, has_side_effects=True, vmem_limit_bytes=60 * 1024 * 1024
        ),
        name="substitution",
    )(
        lower_pattern.transpose(2, 3, 1, 0).reshape(3, 1, NL), upper_pattern.transpose(2, 3, 1, 0).reshape(3, 1, NL), rhs.reshape(NL, 64, 128),
        lower.reshape(blocks), lower_inv.reshape(NL, 128, 128), upper.reshape(blocks), upper_inv.reshape(NL, 128, 128),
    )
    return got.reshape(NL, 1, 64, 128)


def solution(mesh):
    in_specs = (
        P(None, "prow", None, None),
        P(None, "prow", None, "pcol", None, None),
        P(None, "prow", None, "pcol"),
        P(None, "prow", None, None),
        P(None, "prow", None, "pcol", None, None),
        P(None, "prow", None, "pcol"),
        P(None, "prow", None, None),
    )
    out_specs = P(None, "prow", None, None)
    return jax.shard_map(shards, mesh=mesh, in_specs=in_specs, out_specs=out_specs, check_vma=False)
```

```python
import functools

import jax
import jax.numpy as jnp
from jax import lax
from jax.experimental import pallas as pl
from jax.experimental.pallas import tpu as pltpu
from jax.sharding import PartitionSpec as P

MESH = pl.DeviceIdType.MESH
NL = 6
NP = 16
NS = 8
NT = 4
TR = 16
BF16 = jnp.bfloat16
F32 = jnp.float32


def mm_t(x, w):
    return lax.dot_general(
        x, w, (((1,), (1,)), ((), ())),
        precision=lax.Precision.HIGHEST, preferred_element_type=F32,
    )


def mm(a, b):
    return lax.dot_general(
        a, b, (((1,), (0,)), ((), ())),
        precision=lax.Precision.HIGHEST, preferred_element_type=F32,
    )


HELD = {}
for _row, _col in ((5, 4), (4, 5), (3, 4), (2, 3), (1, 3), (0, 3), (1, 2), (0, 2), (0, 1)):
    HELD[_row, _col] = (sum(n for _, n in HELD.values()), min(NP, 1 << _col))
NHELD = sum(n for _, n in HELD.values())
GROUP = {key: i for i, key in enumerate(HELD)}
GATHERED = {"x4": (0, 16), "z5": (16, 16), "z4": (32, 16), "z3": (48, 8), "z2": (56, 4), "z1": (60, 2)}
STEP = {key: i for i, key in enumerate(GATHERED)}
NGATHERED = 62


def split(x):
    high = x.astype(BF16)
    return high, (x - high.astype(F32)).astype(BF16)


def dot_t(x, w):
    return lax.dot_general(x, w, (((1,), (1,)), ((), ())), preferred_element_type=F32)


def width(level):
    return min(NP, 1 << level)


def kernel(
    lpat, upat, rhs_h, low_h, linv_h, upp_h, uinv_h, out,
    rhs, low, linv, upp, uinv, mf, mb, accf, accb, xf, xb, pf, ca, cb, own,
    e1, m21, held, wh, wl, seen, mine, r4, r5, r45, d3, d5, d4,
    s_in, s_x, s_z, s_ca, s_cb, s_held, s_seen, s_rows, s_out, s_e1, t_e1, s_m21, t_m21,
    t_x0, t_a, t_b, t_ag, t_held, t_seen, t_rows, t_z, t_out,
):
    r = lax.axis_index("prow")
    c = lax.axis_index("pcol")
    par, q = c // NP, lax.rem(c, NP)
    even, odd = par == 0, par == 1
    dy = lax.rem(r // 2 - q // 2 + 9, 8)
    owner = dy < 4
    slot = jnp.where(owner, dy * 2 + lax.rem(r, 2), 0)
    diag = r == q

    def seat(k, row):
        return 8 * (2 * lax.rem(k, 2) + lax.rem(row, 2)) + 4 * (k // 2) + 2 * lax.rem(k, 2)

    def tail_seat(k, row):
        return seat(k, row) + 1

    col_x, col_z = c // 8, lax.rem(c, 8)
    half = col_x // 2
    turned = lax.rem(col_z + 8 - 2 * half, 8)
    team = jnp.logical_and(lax.rem(col_x, 2) == lax.rem(r, 2), lax.rem(turned, 4) == 0)
    k_tail = half + 2 * (turned // 4)
    tail = c == tail_seat(k_tail, r)
    k_me = jnp.where(tail, k_tail, jnp.where(team, half + 2 * (turned // 4), 0))

    def same(level):
        return r // width(level) == q // width(level)

    def near(position, j):
        return lax.rem(position // 2 + j // 2 + 7, 8) * 2 + lax.rem(j, 2)

    def at(row, col):
        return {"prow": row, "pcol": col}

    barrier = pltpu.get_barrier_semaphore()

    def tell(row, col):
        @pl.when(jnp.logical_not(jnp.logical_and(row == r, col == c)))
        def _():
            pl.semaphore_signal(barrier, inc=1, device_id=at(row, col), device_id_type=MESH)

    @pl.when(owner)
    def _():
        @pl.loop(0, 2 * NP)
        def _(k):
            tell(q, k)

    @pl.loop(0, NT)
    def _(k):
        tell(r, seat(k, r))
        tell(r, tail_seat(k, r))

    @pl.loop(0, NS)
    def _(j):
        tell(near(q, j), c)

    @pl.when(jnp.logical_and(even, same(2)))
    def _():
        tell(r, NP + q)

    @pl.when(jnp.logical_or(team, tail))
    def _():
        @pl.loop(0, 2 * NP)
        def _(k):
            tell(r, k)

    @pl.when(team)
    def _():
        @pl.loop(0, NP)
        def _(k):
            tell(k, seat(k_me, k))

    @pl.when(tail)
    def _():
        @pl.loop(0, 8)
        def _(d):
            row = jnp.bitwise_xor(r, d)
            tell(row, seat(k_me, row))

        @pl.loop(1, 4)
        def _(d):
            row = jnp.bitwise_xor(r, d)
            tell(row, tail_seat(k_me, row))

    loads = [(rhs_h, rhs), (linv_h, linv), (uinv_h, uinv)]
    for m in range(3):
        loads.append((low_h.at[pl.ds(2 * m + 1, 5 - 2 * m), m], low.at[pl.ds(2 * m + 1, 5 - 2 * m), m]))
    for m in range(3):
        loads.append((upp_h.at[pl.ds(0, 2 * m + 1), m], upp.at[pl.ds(0, 2 * m + 1), m]))
    copies = [pltpu.make_async_copy(a, b, s_in.at[i]) for i, (a, b) in enumerate(loads)]
    for copy in copies:
        copy.start()

    accf[...] = jnp.zeros_like(accf)
    accb[...] = jnp.zeros_like(accb)
    def fold(inv, block, bit):
        return mm(inv, block * bit.astype(F32))

    for i in (0, 1, 3):
        copies[i].wait()
    for row in (1, 2):
        mf[row, 0] = fold(linv[row], low[row, 0], lpat[0, 0, row])

    @pl.when(jnp.logical_and(diag, even))
    def _():
        for row in (1, 2):
            accf[row] = mm_t(rhs[row], linv[row]).reshape(NS, 8, 128)
        xf[0] = mm_t(rhs[0], linv[0]).reshape(NS, 8, 128)

    def prepare_forward():
        top = mm(uinv[5], linv[5])
        for m in range(2):
            for row in range(3, NL):
                mf[row, m] = fold(top if row == 5 else linv[row], low[row, m], lpat[m, 0, row])

        @pl.when(diag)
        def _():
            for row in range(3, NL):
                @pl.when(par == (row - 1) % 2)
                def _(row=row):
                    accf[row] = mm_t(rhs[row], top if row == 5 else linv[row]).reshape(NS, 8, 128)

    one = jnp.where(diag, 1, 0)
    seats = 2 * NT - jnp.where(jnp.logical_or(team, tail), 1, 0)
    expected = 2 * NS - one + jnp.where(owner, NP - 1, 0) + seats
    expected = expected + jnp.where(team, 2 * NP - 1 + NP - 1 + 8, 0)
    expected = expected + jnp.where(tail, 2 * NP - 1 + 3, 0)
    expected = expected + jnp.where(jnp.logical_and(odd, same(2)), 1, 0)
    pl.semaphore_wait(barrier, expected)

    def wait_bytes(ref, sem):
        pltpu.make_async_copy(ref, ref, sem).wait()

    def push(source, target, send_sem, recv_sem, row, col, may_be_me):
        def remote():
            pltpu.make_async_remote_copy(
                source, target, send_sem, recv_sem, device_id=at(row, col), device_id_type=MESH
            ).start()

        if not may_be_me:
            remote()
            return
        me = jnp.logical_and(row == r, col == c)
        pl.when(jnp.logical_not(me))(remote)

        @pl.when(me)
        def _():
            pltpu.make_async_copy(source, target, recv_sem).start()

    @pl.when(jnp.logical_and(diag, even))
    def _():
        @pl.loop(1, NP)
        def _(d):
            push(xf.at[0], xf.at[0], t_x0.at[d], s_x.at[0], jnp.bitwise_xor(r, d), c, False)

    def to_owners(source, target, place, send_sem, recv_sem, parity):
        for j in (6, 7, 0, 1, 4, 5, 2, 3):
            push(source.at[j], target.at[place], send_sem, recv_sem, near(r, j), parity * NP + r, parity is par)

    def to_team(piece, target, send_sem, recv_sem, where):
        for k in range(NT):
            push(piece(pl.ds(2 * k, 2)), target, send_sem, recv_sem, r, where(k, r), True)

    def wait_slices(ref, sem):
        @pl.when(owner)
        def _():
            wait_bytes(ref.at[pl.ds(0, NS - 1)], sem)

        @pl.when(jnp.logical_not(owner))
        def _():
            wait_bytes(ref, sem)

    def give(row, col, source):
        first, n = HELD[row, col]
        i = GROUP[row, col]
        where = seat if row > 2 else tail_seat

        @pl.when(same(col))
        def _():
            @pl.loop(0, NT)
            def _(k):
                push(source, held.at[first + lax.rem(q, n)], t_held.at[i], s_held.at[i], r, where(k, r), True)

    def minus(ref, row, x, w):
        ref[row] = ref[row] - mm_t(x, w).reshape(NS, 8, 128)

    def forward_hold(level):
        m = level // 2
        if level == 0:
            @pl.when(jnp.logical_not(diag))
            def _():
                wait_bytes(xf.at[0], s_x.at[0])
        else:
            wait_slices(xf.at[level], s_x.at[level])
        x = xf[level].reshape(64, 128)
        if level < 3:
            if level != 1:
                @pl.when(same(level + 1))
                def _():
                    row = level + 1
                    pf[level] = accf[row] - mm_t(x, mf[row, m]).reshape(NS, 8, 128)
                    if level == 0:
                        for d in range(4):
                            push(
                                pf.at[0], e1.at[lax.rem(q, 2)], t_e1, s_e1,
                                jnp.bitwise_xor(r, d), r, True,
                            )
                    to_owners(
                        pf.at[level], ca, row * NP + lax.rem(q, width(row)), t_a.at[row], s_ca.at[row], 1 - par
                    )

            if level == 0:
                prepare_forward()
            row = level + 2
            if row < 4:
                @pl.when(same(row))
                def _():
                    minus(accf, row, x, mf[row, m])
                    if row == 3:
                        to_owners(accf.at[row], cb, row * NP + lax.rem(q, width(row)), t_b.at[row], s_cb.at[row], par)

            for row in range(level + 3, 4):
                @pl.when(same(row))
                def _(row=row):
                    minus(accf, row, x, mf[row, m])

            minus(accf, 4, x, mf[4, m])
            minus(accf, 5, x, mf[5, m])
            if level == 2:
                to_team(lambda k: accf.at[pl.ds(4, 2), k], r45.at[q], t_rows.at[0], s_rows.at[0], seat)
        else:
            minus(accf, 4, x, mf[4, m])
            to_team(lambda k: accf.at[4, k], r4.at[q], t_rows.at[1], s_rows.at[1], seat)
            minus(accf, 5, x, mf[5, m])
            to_team(lambda k: accf.at[5, k], r5.at[q], t_rows.at[2], s_rows.at[2], seat)

        @pl.when(diag)
        def _():
            accb[level] = mm_t(x, uinv[level]).reshape(NS, 8, 128)

    def forward_second():
        wait_bytes(e1, s_e1)
        x = (e1[0] + e1[1]).reshape(64, 128)
        wait_bytes(m21, s_m21)
        pf[1] = accf[2] - mm_t(x, m21[...]).reshape(NS, 8, 128)
        to_owners(pf.at[1], ca, 2 * NP + lax.rem(q, 4), t_a.at[2], s_ca.at[2], par)

    def forward_own(level):
        n = width(level)
        wait_bytes(ca.at[pl.ds(level * NP, n)], s_ca.at[level])
        total = jnp.sum(ca[level * NP:level * NP + n], axis=0)
        if level >= 3:
            wait_bytes(cb.at[pl.ds(level * NP, n)], s_cb.at[level])
            total = total + jnp.sum(cb[level * NP:level * NP + n], axis=0)
        own[level] = total
        xf[level, slot] = total

        @pl.loop(1, NP)
        def _(d):
            row = jnp.bitwise_xor(r, NP - d)
            push(own.at[level], xf.at[level, slot], t_ag.at[level], s_x.at[level], row, c, False)

    def prepare_back():
        for m in range(3):
            for row in range(0, min(4, 2 * m + 1)):
                mb[row, m] = fold(uinv[row], upp[row, m], upat[m, 0, row])

    def first_wide():
        mf[5, 2] = fold(mm(uinv[5], linv[5]), low[5, 2], lpat[2, 0, 5])
        give(5, 4, mf.at[5, 2])

    for i in (2, 4, 5, 6, 7, 8):
        copies[i].wait()

    @pl.when(even)
    def _():
        pl.when(jnp.logical_not(same(2)))(first_wide)
        forward_hold(0)

        @pl.when(same(2))
        def _():
            forward_second()
            first_wide()

        prepare_back()
        pl.when(owner)(functools.partial(forward_own, 2))
        forward_hold(2)
        give(3, 4, mb.at[3, 2])
        give(1, 2, mb.at[1, 1])
        give(0, 2, mb.at[0, 1])

    @pl.when(odd)
    def _():
        @pl.when(same(2))
        def _():
            push(mf.at[2, 0], m21, t_m21, s_m21, r, q, False)

        mb[4, 2] = fold(uinv[4], upp[4, 2], upat[2, 0, 4])
        give(4, 5, mb.at[4, 2])
        prepare_forward()
        prepare_back()
        pl.when(owner)(functools.partial(forward_own, 1))
        forward_hold(1)
        give(2, 3, mb.at[2, 1])
        give(1, 3, mb.at[1, 1])
        pl.when(owner)(functools.partial(forward_own, 3))
        forward_hold(3)
        give(0, 3, mb.at[0, 1])
        give(0, 1, mb.at[0, 0])

    def take(row, col):
        first, n = HELD[row, col]
        wait_bytes(held.at[pl.ds(first, n)], s_held.at[GROUP[row, col]])
        for i in range(first // 2, (first + n) // 2):
            high, low_ = split(jnp.concatenate([held[2 * i], held[2 * i + 1]], axis=1))
            wh[i] = high
            wl[i] = low_

    def apply(row, col, name):
        first, n = HELD[row, col]
        base, _ = GATHERED[name]
        total = jnp.zeros((TR, 128), F32)
        for i in range(n // 2):
            high, low_ = split(jnp.concatenate(
                [seen[base + 2 * i].reshape(TR, 128), seen[base + 2 * i + 1].reshape(TR, 128)], axis=1
            ))
            both = dot_t(jnp.concatenate([high, low_], axis=0), wh[first // 2 + i])
            total = total + both[0:TR] + both[TR:2 * TR] + dot_t(high, wl[first // 2 + i])
        return total

    def gather(name, value):
        base, n = GATHERED[name]
        i = STEP[name]
        where = seat if n == NP else tail_seat
        mine[i] = value.reshape(2, 8, 128)
        place = base + lax.rem(r, n)
        if name != "z3":
            seen[place] = value.reshape(2, 8, 128)

        @pl.loop(0 if name == "z3" else 1, n)
        def _(d):
            row = jnp.bitwise_xor(r, n - 1 - d if name == "z3" else n - d)
            push(mine.at[i], seen.at[place], t_seen.at[i], s_seen.at[i], row, where(k_me, row), False)

    def gathered(name):
        base, n = GATHERED[name]
        wait_bytes(seen.at[pl.ds(base, n if name == "z3" else n - 1)], s_seen.at[STEP[name]])

    def to_holders(level, name):
        @pl.loop(0, NP)
        def _(d):
            row = jnp.bitwise_xor(r, NP - 1 - d)
            push(
                mine.at[STEP[name]], xb.at[level, pl.ds(2 * k_me, 2)], t_z.at[level], s_z.at[level],
                row, (level % 2) * NP + r, True,
            )

    def deliver(level, source, n):
        @pl.loop(0, 2 * NP)
        def _(col):
            push(source, out.at[pl.ds(level, n), pl.ds(2 * k_me, 2)], t_out.at[level], s_out, r, col, True)

    def deliver_far_first(level, source):
        target = out.at[pl.ds(level, 1), pl.ds(2 * k_me, 2)]
        for dx in (2, 1, 3, 0):
            for dz in (4, 3, 5, 2, 6, 1, 7, 0):
                if dx == dz == 0:
                    pltpu.make_async_copy(source, target, s_out).start()
                else:
                    col = 8 * lax.rem(col_x + dx, 4) + lax.rem(col_z + dz, 8)
                    push(source, target, t_out.at[level], s_out, r, col, False)

    @pl.when(team)
    def _():
        wait_bytes(r45, s_rows.at[0])
        before = jnp.sum(r45[...], axis=0).reshape(2, TR, 128)
        wait_bytes(r4, s_rows.at[1])
        x4 = jnp.sum(r4[...], axis=0).reshape(TR, 128) + before[0]
        gather("x4", x4)
        take(5, 4)
        u4 = mm_t(x4, uinv[4])
        wait_bytes(r5, s_rows.at[2])
        z5 = jnp.sum(r5[...], axis=0).reshape(TR, 128) + before[1]
        gathered("x4")
        z5 = z5 - apply(5, 4, "x4")
        gather("z5", z5)
        to_holders(5, "z5")
        deliver(5, mine.at[pl.ds(STEP["z5"], 1)], 1)
        take(4, 5)
        gathered("z5")
        z4 = u4 - apply(4, 5, "z5")
        gather("z4", z4)
        to_holders(4, "z4")
        deliver(4, mine.at[pl.ds(STEP["z4"], 1)], 1)
        take(3, 4)

    @pl.when(odd)
    def _():
        wait_bytes(xb.at[5], s_z.at[5])
        z = xb[5].reshape(64, 128)
        minus(accb, 3, z, mb[3, 2])
        to_team(lambda k: accb.at[3, k], d3.at[q], t_rows.at[3], s_rows.at[3], seat)
        for row in range(3):
            minus(accb, row, z, mb[row, 2])
        to_team(lambda k: accb.at[pl.ds(0, 3), k], d5.at[q], t_rows.at[4], s_rows.at[4], tail_seat)

    @pl.when(team)
    def _():
        wait_bytes(d3, s_rows.at[3])
        z3 = jnp.sum(d3[...], axis=0).reshape(TR, 128)
        gathered("z4")
        z3 = z3 - apply(3, 4, "z4")
        gather("z3", z3)
        deliver(3, mine.at[pl.ds(STEP["z3"], 1)], 1)

    @pl.when(even)
    def _():
        wait_bytes(xb.at[4], s_z.at[4])
        z = xb[4].reshape(64, 128)
        minus(accb, 2, z, mb[2, 2])
        to_team(lambda k: accb.at[2, k], d4.at[q, 2], t_rows.at[6], s_rows.at[6], tail_seat)
        for row in range(2):
            minus(accb, row, z, mb[row, 2])
        to_team(lambda k: accb.at[pl.ds(0, 2), k], d4.at[q, pl.ds(0, 2)], t_rows.at[5], s_rows.at[5], tail_seat)

    @pl.when(tail)
    def _():
        take(2, 3)
        take(1, 3)
        take(1, 2)
        wait_bytes(d5, s_rows.at[4])
        late = jnp.sum(d5[...], axis=0).reshape(3, TR, 128)
        gathered("z3")
        late2 = late[2] - apply(2, 3, "z3")
        late1 = late[1] - apply(1, 3, "z3")
        take(0, 3)
        take(0, 2)
        take(0, 1)
        late0 = late[0] - apply(0, 3, "z3")
        wait_bytes(r4, s_rows.at[6])
        gather("z2", late2 + jnp.sum(d4[:, 2], axis=0).reshape(TR, 128))
        deliver(2, mine.at[pl.ds(STEP["z2"], 1)], 1)
        wait_bytes(r45, s_rows.at[5])
        last = jnp.sum(d4[:, 0:2], axis=0).reshape(2, TR, 128)
        late0 = late0 + last[0]
        gathered("z2")
        gather("z1", late1 + last[1] - apply(1, 2, "z2"))
        late0 = late0 - apply(0, 2, "z2")
        deliver_far_first(1, mine.at[pl.ds(STEP["z1"], 1)])
        gathered("z1")
        mine[6] = (late0 - apply(0, 1, "z1")).reshape(2, 8, 128)
        deliver_far_first(0, mine.at[pl.ds(6, 1)])

    @pl.when(jnp.logical_and(diag, even))
    def _():
        @pl.loop(1, NP)
        def _(d):
            wait_bytes(xf.at[0], t_x0.at[d])

    def slices(n):
        return ca.at[pl.ds(0, n)]

    def sent_slices(sem, n):
        @pl.when(diag)
        def _():
            wait_bytes(slices(n - 1), sem)

        @pl.when(jnp.logical_not(diag))
        def _():
            wait_bytes(slices(n), sem)

    @pl.when(jnp.logical_and(even, same(1)))
    def _():
        wait_bytes(slices(NS), t_a.at[1])

        @pl.when(diag)
        def _():
            wait_bytes(xf.at[pl.ds(0, 3)], t_e1)

        @pl.when(jnp.logical_not(diag))
        def _():
            wait_bytes(xf.at[pl.ds(0, 4)], t_e1)

    @pl.when(jnp.logical_and(even, same(2)))
    def _():
        sent_slices(t_a.at[2], NS)

    @pl.when(jnp.logical_and(even, same(3)))
    def _():
        wait_bytes(slices(NS), t_a.at[3])

    @pl.when(jnp.logical_and(odd, same(2)))
    def _():
        wait_bytes(m21, t_m21)

    @pl.when(jnp.logical_and(odd, same(3)))
    def _():
        sent_slices(t_b.at[3], NS)

    for row in range(1, 4):
        @pl.when(jnp.logical_and(par == row % 2, owner))
        def _(row=row):
            wait_bytes(slices(NP - 1), t_ag.at[row])

    def sent_rows(i, n):
        kept = tail if i > 3 else team

        @pl.when(kept)
        def _():
            wait_bytes(slices(2 * (NT - 1) * n), t_rows.at[i])

        @pl.when(jnp.logical_not(kept))
        def _():
            wait_bytes(slices(2 * NT * n), t_rows.at[i])

    def sent_blocks(row, col):
        @pl.when(same(col))
        def _():
            i = GROUP[row, col]
            kept = team if row > 2 else tail

            @pl.when(kept)
            def _():
                wait_bytes(held.at[pl.ds(0, NT - 1)], t_held.at[i])

            @pl.when(jnp.logical_not(kept))
            def _():
                wait_bytes(held.at[pl.ds(0, NT)], t_held.at[i])

    @pl.when(even)
    def _():
        sent_rows(0, 2)
        sent_rows(5, 2)
        sent_rows(6, 1)
        for key in ((5, 4), (3, 4), (1, 2), (0, 2)):
            sent_blocks(*key)

    @pl.when(odd)
    def _():
        sent_rows(1, 1)
        sent_rows(2, 1)
        sent_rows(3, 1)
        sent_rows(4, 3)
        for key in ((4, 5), (2, 3), (1, 3), (0, 3), (0, 1)):
            sent_blocks(*key)

    @pl.when(team)
    def _():
        for name in ("x4", "z5", "z4"):
            wait_bytes(slices(2 * (NP - 1)), t_seen.at[STEP[name]])
        wait_bytes(slices(2 * 8), t_seen.at[STEP["z3"]])
        for level in (5, 4):
            own_seat = jnp.logical_and(diag, par == level % 2)

            @pl.when(own_seat)
            def _(level=level):
                wait_bytes(slices(2 * (NP - 1)), t_z.at[level])

            @pl.when(jnp.logical_not(own_seat))
            def _(level=level):
                wait_bytes(slices(2 * NP), t_z.at[level])
        for level in (5, 4, 3):
            wait_bytes(slices(2 * (2 * NP - 1)), t_out.at[level])

    @pl.when(tail)
    def _():
        wait_bytes(slices(2 * 3), t_seen.at[STEP["z2"]])
        wait_bytes(slices(2 * 1), t_seen.at[STEP["z1"]])
        for level in (2, 1, 0):
            wait_bytes(slices(2 * (2 * NP - 1)), t_out.at[level])

    wait_bytes(out, s_out)


def shards(rhs, lower, lower_pattern, lower_inv, upper, upper_pattern, upper_inv):
    v = pltpu.VMEM
    dma = pltpu.SemaphoreType.DMA
    slices = (NL, NS, 8, 128)
    parts = (NL * NP, 8, 128)
    blocks = (NL, 3, 128, 128)
    got = pl.pallas_call(
        kernel,
        out_shape=jax.ShapeDtypeStruct(slices, F32),
        in_specs=[pl.BlockSpec(memory_space=pltpu.SMEM)] * 2 + [pl.BlockSpec(memory_space=pl.ANY)] * 5,
        out_specs=pl.BlockSpec(memory_space=pltpu.VMEM),
        scratch_shapes=[
            v((NL, 64, 128), F32), v(blocks, F32), v((NL, 128, 128), F32), v(blocks, F32), v((NL, 128, 128), F32),
            v(blocks, F32), v(blocks, F32), v(slices, F32), v(slices, F32), v(slices, F32), v(slices, F32),
            v(slices, F32), v(parts, F32), v(parts, F32), v((NL, 8, 128), F32),
            v((2, NS, 8, 128), F32), v((128, 128), F32), v((NHELD, 128, 128), F32), v((NHELD // 2, 128, 256), BF16), v((NHELD // 2, 128, 256), BF16),
            v((NGATHERED, 2, 8, 128), F32), v((7, 2, 8, 128), F32),
            v((NP, 2, 8, 128), F32), v((NP, 2, 8, 128), F32), v((NP, 2, 2, 8, 128), F32),
            v((NP, 2, 8, 128), F32), v((NP, 3, 2, 8, 128), F32), v((NP, 3, 2, 8, 128), F32),
            dma((9,)), dma((NL,)), dma((NL,)), dma((NL,)), dma((NL,)), dma((len(HELD),)), dma((len(GATHERED),)), dma((7,)), dma, dma, dma, dma, dma,
            dma((NP,)), dma((NL,)), dma((NL,)), dma((NL,)), dma((len(HELD),)), dma((len(GATHERED),)), dma((7,)),
            dma((NL,)), dma((NL,)),
        ],
        compiler_params=pltpu.CompilerParams(
            collective_id=0, has_side_effects=True, vmem_limit_bytes=60 * 1024 * 1024
        ),
        name="substitution",
    )(
        lower_pattern.transpose(2, 3, 1, 0).reshape(3, 1, NL), upper_pattern.transpose(2, 3, 1, 0).reshape(3, 1, NL), rhs.reshape(NL, 64, 128),
        lower.reshape(blocks), lower_inv.reshape(NL, 128, 128), upper.reshape(blocks), upper_inv.reshape(NL, 128, 128),
    )
    return got.reshape(NL, 1, 64, 128)


def solution(mesh):
    in_specs = (
        P(None, "prow", None, None),
        P(None, "prow", None, "pcol", None, None),
        P(None, "prow", None, "pcol"),
        P(None, "prow", None, None),
        P(None, "prow", None, "pcol", None, None),
        P(None, "prow", None, "pcol"),
        P(None, "prow", None, None),
    )
    out_specs = P(None, "prow", None, None)
    return jax.shard_map(shards, mesh=mesh, in_specs=in_specs, out_specs=out_specs, check_vma=False)
```
